512 devices in a mesh: dp: 16 (over x, z_hi, core), expert: 32 (over z_lo, y).
Axes of the slice: x: 4, y: 4, z: 16 (z_hi: 2, z_lo: 8; z = z_hi * 8 + z_lo), core: 2. Of those that a mesh axis runs over, the one named last changes fastest.
Arguments:
- stash: bfloat16 [512, 5120], P('dp', 'expert'), may hold values from -6 to 6
- scale_exp: int32 [512, 160], P('dp', 'expert'), may hold values from -2 to 1
- grad_out: bfloat16 [512, 5120], P('dp', 'expert'), may hold values from -6 to 6
- route_ids: int32 [512, 6], P('dp'), may hold values from 0 to 15, all different within a row; in each aligned block of 16 rows (0 to 15, 16 to 31, ...) at most 8 rows name the same one
- route_probs: bfloat16 [512, 6], P('dp'), may hold values from 0.049804688 to 0.5
- w_gate: bfloat16 [16, 7864320], P(None, ('dp', 'expert')), may hold values from -0.078125 to 0.078125
- w_up: bfloat16 [16, 7864320], P(None, ('dp', 'expert')), may hold values from -0.078125 to 0.078125
- w_down: bfloat16 [16, 7864320], P(None, ('dp', 'expert')), may hold values from -0.15625 to 0.15625
Outputs:
- grad_in: bfloat16 [512, 5120], P('dp', 'expert')
- grad_probs: float32 [512, 6], P('dp')
- grad_gate: bfloat16 [16, 7864320], P(None, ('dp', 'expert'))
- grad_up: bfloat16 [16, 7864320], P(None, ('dp', 'expert'))
- grad_down: bfloat16 [16, 7864320], P(None, ('dp', 'expert'))
The draws below stay inside these ranges and needn't reach their ends.
Inputs may be any that keep to these rules, and one draw needn't show every extreme that they name: `route_ids`: each row names 6 different experts; within each aligned block of 16 rows (the blocks of one shard in order) no expert is named by more than 8 rows, a bound that some block reaches.
All inputs are finite; a program needn't handle non-finite values.
Results may differ from the reference program's by a relative error of at most 0.022.
Values may be sent and summed in bfloat16 or wider, within the bound.
No kernel may reach another device: no remote copies, remote signals or barrier semaphores. Data moves between devices by JAX's collectives and lax.ppermute only.
A program may use at most 64 MiB of HBM per device.

```python
import math
import jax
import jax.numpy as jnp
import numpy as np
from jax import lax

D = 5120
FF = 1536
K = 6
BLK = 16
EXPERTS = 16
REPL = 2
TOK_DP = 32
TOKENS = 512
CAP = 8
DSH = 160
FSH = 96
TILE = 15360
N_DP = 16
N_EXPERT = 32


def set_ends(result, key, low, largest):
    shape = result.shape
    index_at = [jax.random.randint(jax.random.fold_in(key, axis), (), 0, shape[axis]) for axis in range(len(shape))]
    result = result.at[tuple(index_at)].set(low)
    longest = shape.index(max(shape))
    index_at[longest] = (index_at[longest] + 1) % shape[longest]
    return result.at[tuple(index_at)].set(largest)


def block_levels(rng, extent, cuts, low, top_value):
    def one(axis_at, shards_of):
        steps = jax.random.uniform(jax.random.fold_in(jax.random.fold_in(rng, 6), axis_at), (shards_of,), jnp.float32, low / len(cuts), top_value / len(cuts))
        return jnp.repeat(jnp.exp(steps), extent[axis_at] // shards_of).reshape((-1,) + (1,) * (len(extent) - axis_at - 1))

    loudness = one(*cuts[0])
    for cut in cuts[1:]:
        loudness = loudness * one(*cut)
    return loudness


def routed_block(stream_key, own, number, rows, number_of, top, most, lean):
    ranking = jax.random.permutation(stream_key, number_of)
    crowded, common = portions_of(number_of, rows * top, most, lean, True), portions_of(number_of, rows * top, most, lean, False)
    places = jnp.arange(number_of)

    def named(lengths, turn):
        used = int((lengths > 0).sum())
        fixed = max(1, used // 4)
        moved = fixed + (places - fixed + turn * (used - fixed)) % max(1, number_of - fixed)
        return jnp.zeros((number_of,), jnp.int32).at[ranking[jnp.where(places < fixed, places, moved)]].set(jnp.asarray(lengths, jnp.int32))

    lengths = jnp.where(number % 4 == 0, named(crowded, number // 4), named(common, number - number // 4 - 1))
    mixed = jax.random.permutation(jax.random.fold_in(own, 3), number_of)
    source_of, sink = mixed[0:number_of // 2 * 2:2], mixed[1:number_of // 2 * 2:2]
    slack = jnp.minimum(lengths[source_of] - 1, most - lengths[sink]) // 2
    slack = jnp.where((source_of == ranking[0]) | (sink == ranking[0]) | (lengths[sink] == 0), 0, jnp.maximum(slack, 0))
    moved = jax.random.randint(jax.random.fold_in(own, 4), (number_of // 2,), 0, 1 << 20) % (slack + 1)
    lengths = lengths.at[source_of].add(-moved).at[sink].add(moved)
    labels = jnp.searchsorted(jnp.cumsum(lengths), jnp.arange(rows * top), side="right").astype(jnp.int32)
    table = labels.reshape(top, rows).T
    table = table[jax.random.permutation(jax.random.fold_in(own, 1), rows)]
    turn = jax.random.randint(jax.random.fold_in(own, 2), (rows, 1), 0, top)
    return jnp.take_along_axis(table, (jnp.arange(top)[None, :] + turn) % top, axis=1)


def portions_of(count, total, bound, slope, full):
    portions = [(1 << 20) // math.isqrt(rank ** slope) + 1 for rank in range(1, count + 1)]
    largest = bound if full else min(bound, max(-(-total // count), total * portions[0] // sum(portions)))
    least = 1 if total - largest >= count - 1 else 0
    holding, spare = [largest] + [least] * (count - 1), total - largest - least * (count - 1)
    while spare > 0:
        candidates = [i for i in range(1, count) if holding[i] < largest] or [i for i in range(1, count) if holding[i] < bound]
        pool, left = sum([portions[i] for i in candidates]), spare
        for i in candidates:
            more = min(bound - holding[i], max(1, left * portions[i] // pool), spare)
            holding[i] = holding[i] + more
            spare = spare - more
    return np.array(holding)


def centred(own_key, dims, deviation, most, pieces=(), held_as=jnp.bfloat16):
    values = jax.random.normal(own_key, dims, jnp.float32) * deviation
    if len(pieces) > 0:
        values = block_levels(own_key, dims, pieces, -0.22, 0.18) * values
    return jnp.clip(values, min=-most, max=most).astype(held_as)


def setup_inputs(seed: int = 0) -> dict:
    key_list = jax.random.split(jax.random.key(seed), 9)
    stash = centred(key_list[0], (TOKENS, D), 1.0, 6.0, ((0, 16), (1, 32)))
    scale_exp = set_ends(jax.random.randint(key_list[1], (TOKENS, D // 32), -2, 2), jax.random.fold_in(key_list[1], 1), -2, 1).astype(jnp.int32)
    grad_out = centred(key_list[2], (TOKENS, D), 1.0, 6.0, ((0, 16), (1, 32)))
    route_ids_keys = jax.random.split(jax.random.fold_in(key_list[3], 1), TOKENS // BLK)
    route_ids_turns = jax.random.permutation(jax.random.fold_in(key_list[3], 3), TOKENS // BLK)
    route_ids = jax.vmap(lambda own, number: routed_block(jax.random.fold_in(key_list[3], 2), own, number, BLK, EXPERTS, K, CAP, 2))(route_ids_keys, route_ids_turns).reshape((TOKENS, K))
    route_probs = jnp.clip(0.049804688 + 0.4501953 * jax.random.uniform(key_list[4], (TOKENS, K), jnp.float32) ** block_levels(key_list[4], (TOKENS, K), ((0, 16),), -0.2, 0.2), 0.049804688, 0.5).astype(jnp.bfloat16)
    w_gate = centred(key_list[5], (EXPERTS, N_DP * N_EXPERT * TILE), D ** -0.5, 0.078125, ((1, 512),))
    w_up = centred(key_list[6], (EXPERTS, N_DP * N_EXPERT * TILE), D ** -0.5, 0.078125, ((1, 512),))
    w_down = centred(key_list[7], (EXPERTS, N_DP * N_EXPERT * TILE), FF ** -0.5, 0.15625, ((1, 512),))
    return dict(stash=stash, scale_exp=scale_exp, grad_out=grad_out, route_ids=route_ids, route_probs=route_probs, w_gate=w_gate, w_up=w_up, w_down=w_down)


scale_cols = 32


def round_keep(value):
    rounded = lax.optimization_barrier(value.astype(jnp.bfloat16))
    return rounded.astype(jnp.float32)


def untile(stored):
    blocks = stored.reshape(EXPERTS, N_DP, N_EXPERT, DSH, FSH)
    return jnp.transpose(blocks, (0, 2, 3, 1, 4)).reshape(EXPERTS, D, FF)


def retile(matrix):
    blocks = matrix.reshape(EXPERTS, N_EXPERT, DSH, N_DP, FSH)
    return jnp.transpose(blocks, (0, 3, 1, 2, 4)).reshape(EXPERTS, N_DP * N_EXPERT * TILE)


def reference(stash, scale_exp, grad_out, route_ids, route_probs, w_gate, w_up, w_down):
    w_gate = untile(w_gate)
    w_up = untile(w_up)
    w_down = untile(w_down)
    factors = jnp.repeat(jnp.exp2(scale_exp.astype(jnp.float32)), scale_cols, axis=1)
    inputs = (stash.astype(jnp.float32) * factors).astype(jnp.bfloat16)
    rows_max = TOKENS * CAP // BLK
    slices = N_DP
    slice_width = FF // N_DP
    positions = jnp.arange(TOKENS)
    block_of = (positions % TOK_DP) // BLK

    def per_expert(carry, expert):
        dx_total, prob_total = carry
        match = route_ids == expert
        hit = jnp.any(match, axis=1)
        weight = jnp.sum(jnp.where(match, route_probs.astype(jnp.float32), 0.0), axis=1)
        index = jnp.nonzero(hit, size=rows_max, fill_value=0)[0]
        valid = (jnp.arange(rows_max) < jnp.sum(hit.astype(jnp.int32))).astype(jnp.float32)
        rows_x = inputs[index]
        rows_dy = grad_out[index]
        gate = (weight[index] * valid)[:, None]
        gate_w = lax.dynamic_index_in_dim(w_gate, expert, 0, False)
        up_w = lax.dynamic_index_in_dim(w_up, expert, 0, False)
        down_w = lax.dynamic_index_in_dim(w_down, expert, 0, False)
        pre_a = jnp.dot(rows_x, gate_w, preferred_element_type=jnp.float32)
        pre_b = jnp.dot(rows_x, up_w, preferred_element_type=jnp.float32)
        back = lax.dot_general(rows_dy, down_w, (((1,), (0,)), ((), ())), preferred_element_type=jnp.float32)
        sig = jax.nn.sigmoid(pre_a)
        act = pre_a * sig
        hidden = act * pre_b
        dh = gate * back
        d_gate = (dh * pre_b * sig * (1.0 + pre_a * (1.0 - sig))).astype(jnp.bfloat16)
        d_up = (dh * act).astype(jnp.bfloat16)
        gated = (gate * hidden).astype(jnp.bfloat16)
        dg3 = d_gate.astype(jnp.float32).reshape(rows_max, slices, slice_width)
        du3 = d_up.astype(jnp.float32).reshape(rows_max, slices, slice_width)
        wg3 = gate_w.astype(jnp.float32).reshape(D, slices, slice_width)
        wu3 = up_w.astype(jnp.float32).reshape(D, slices, slice_width)
        dx_slices = jnp.einsum("rsf,dsf->rsd", dg3, wg3) + jnp.einsum("rsf,dsf->rsd", du3, wu3)
        dx_rows = jnp.sum(round_keep(dx_slices), axis=1) * valid[:, None]
        prob_slices = jnp.sum((hidden * back).reshape(rows_max, slices, slice_width), axis=2)
        prob_rows = jnp.sum(round_keep(prob_slices), axis=1) * valid
        dx_total = dx_total.at[index].add(dx_rows)
        token_val = jnp.zeros((TOKENS,), jnp.float32).at[index].add(prob_rows)
        prob_total = prob_total + jnp.where(match, token_val[:, None], 0.0)
        row_block = block_of[index]
        grad_g = jnp.zeros((D, FF), jnp.float32)
        grad_u = jnp.zeros((D, FF), jnp.float32)
        grad_d = jnp.zeros((D, FF), jnp.float32)
        for block in range(REPL):
            inside = (row_block == block)[:, None]
            part_g = jnp.where(inside, d_gate, jnp.zeros_like(d_gate))
            part_u = jnp.where(inside, d_up, jnp.zeros_like(d_up))
            part_d = jnp.where(inside, gated, jnp.zeros_like(gated))
            contract = (((0,), (0,)), ((), ()))
            grad_g = grad_g + round_keep(lax.dot_general(rows_x, part_g, contract, preferred_element_type=jnp.float32))
            grad_u = grad_u + round_keep(lax.dot_general(rows_x, part_u, contract, preferred_element_type=jnp.float32))
            grad_d = grad_d + round_keep(lax.dot_general(rows_dy, part_d, contract, preferred_element_type=jnp.float32))
        outs = (grad_g.astype(jnp.bfloat16), grad_u.astype(jnp.bfloat16), grad_d.astype(jnp.bfloat16))
        return (dx_total, prob_total), outs

    start = (jnp.zeros((TOKENS, D), jnp.float32), jnp.zeros((TOKENS, K), jnp.float32))
    (dx_total, prob_total), grads = lax.scan(per_expert, start, jnp.arange(EXPERTS))
    return (dx_total.astype(jnp.bfloat16), prob_total, retile(grads[0]), retile(grads[1]), retile(grads[2]))
```

```python
import jax
import jax.numpy as jnp
from jax import lax
from jax.experimental import pallas as pl
from jax.experimental.pallas import tpu as pltpu
from jax.sharding import Mesh, PartitionSpec as P

DP = ("x", "zh", "core")
EX = ("zl", "y")
BLK = 16
TOP = 6
EXPERTS = 16
DSH = 160
FSH = 96
TOKENS = 512
BLOCKS = TOKENS // BLK
ROWS = BLK * TOP
LANES = 128
PACK = TOP * 3 * FSH
COLS = 384
IDS_AT = 2 * DSH
PROBS_AT = IDS_AT + TOP
OUT_COLS = 256
VMEM = 56 * 1024 * 1024


def build_pick(xin_ref, pick_ref):
    ids = xin_ref[:, IDS_AT:IDS_AT + TOP].astype(jnp.float32).astype(jnp.int32)
    token = lax.broadcasted_iota(jnp.int32, (TOKENS, 1), 0) % BLK
    column = lax.broadcasted_iota(jnp.int32, (TOKENS, EXPERTS * BLK), 1)
    for k in range(TOP):
        hot = column == ids[:, k:k + 1] * BLK + token
        hot = jnp.where(hot, 1.0, 0.0).astype(jnp.bfloat16)
        pick_ref[:, k * BLK:(k + 1) * BLK, :] = hot.reshape(BLOCKS, BLK, EXPERTS * BLK)


def forward_kernel(xin_ref, wg_ref, wu_ref, wd_ref, out_ref, pick_ref, dense_ref, rows_ref):
    build_pick(xin_ref, pick_ref)
    x = xin_ref[:, :DSH]
    dy = xin_ref[:, DSH:2 * DSH]

    def expert(e, _):
        at = pl.ds(pl.multiple_of(e * BLK, BLK), BLK)
        for i, (rows, w_ref) in enumerate(((x, wg_ref), (x, wu_ref), (dy, wd_ref))):
            part = jnp.dot(rows, w_ref[e], preferred_element_type=jnp.float32)
            part = part.astype(jnp.bfloat16).reshape(BLOCKS, BLK, FSH)
            dense_ref[:, at, i * LANES:i * LANES + FSH] = part
        return 0

    lax.fori_loop(0, EXPERTS, expert, 0)

    def block(b, _):
        picked = jnp.dot(pick_ref[b], dense_ref[b], preferred_element_type=jnp.float32)
        for k in range(TOP):
            rows_ref[k, pl.ds(pl.multiple_of(b * BLK, BLK), BLK), :] = picked[k * BLK:(k + 1) * BLK]
        return 0

    lax.fori_loop(0, BLOCKS, block, 0, unroll=4)

    def pack(c, _):
        at = pl.ds(pl.multiple_of(c * 64, 64), 64)
        pieces = []
        for k in range(TOP):
            for i in range(3):
                pieces.append(rows_ref[k, at, i * LANES:i * LANES + FSH])
        out_ref[at, :] = jnp.concatenate(pieces, axis=1).astype(jnp.bfloat16)
        return 0

    lax.fori_loop(0, TOKENS // 64, pack, 0)


def backward_kernel(xin_ref, xt_ref, pre_ref, wg_ref, wu_ref, gg_ref, gu_ref, gd_ref, dx_ref,
                    pick_ref, grow_ref, dense_ref, acc_ref):
    build_pick(xin_ref, pick_ref)
    step = 64

    def act(c, _):
        at = pl.ds(pl.multiple_of(c * step, step), step)
        blocks = pl.ds(pl.multiple_of(c * (step // BLK), step // BLK), step // BLK)
        pre = pre_ref[at, :].astype(jnp.float32)
        probs = xin_ref[at, PROBS_AT:PROBS_AT + TOP].astype(jnp.float32)
        sums = []
        for k in range(TOP):
            base = k * 3 * FSH
            a = pre[:, base:base + FSH]
            b = pre[:, base + FSH:base + 2 * FSH]
            back = pre[:, base + 2 * FSH:base + 3 * FSH]
            gate = probs[:, k:k + 1]
            sig = jax.nn.sigmoid(a)
            act_ = a * sig
            hidden = act_ * b
            dh = gate * back
            d_gate = dh * b * sig * (1.0 + a * (1.0 - sig))
            d_up = dh * act_
            gated = gate * hidden
            for i, value in enumerate((d_gate, d_up, gated)):
                value = value.astype(jnp.bfloat16).reshape(step // BLK, BLK, FSH)
                grow_ref[blocks, k * BLK:(k + 1) * BLK, i * LANES:i * LANES + FSH] = value
            sums.append(jnp.sum(hidden * back, axis=1, keepdims=True))
        lane = lax.broadcasted_iota(jnp.int32, (step, LANES), 1)
        tail = jnp.zeros((step, LANES), jnp.float32)
        for k in range(TOP):
            tail = jnp.where(lane == k, sums[k], tail)
        acc_ref[at, OUT_COLS:OUT_COLS + LANES] = tail
        return 0

    lax.fori_loop(0, TOKENS // step, act, 0)

    def block(b, _):
        spread = lax.dot_general(pick_ref[b], grow_ref[b], (((0,), (0,)), ((), ())),
                                 preferred_element_type=jnp.float32)
        dense_ref[b] = spread.astype(jnp.bfloat16)
        return 0

    lax.fori_loop(0, BLOCKS, block, 0, unroll=4)
    acc_ref[:, :OUT_COLS] = jnp.zeros((TOKENS, OUT_COLS), jnp.float32)
    right = (((1,), (1,)), ((), ()))

    def expert(e, _):
        at = pl.ds(pl.multiple_of(e * BLK, BLK), BLK)
        d_gate = dense_ref[:, at, 0:FSH].reshape(TOKENS, FSH)
        d_up = dense_ref[:, at, LANES:LANES + FSH].reshape(TOKENS, FSH)
        gated = dense_ref[:, at, 2 * LANES:2 * LANES + FSH].reshape(TOKENS, FSH)
        xt = xt_ref[:DSH, :]
        dyt = xt_ref[DSH:2 * DSH, :]
        gg_ref[e] = jnp.dot(xt, d_gate, preferred_element_type=jnp.float32).astype(jnp.bfloat16)
        gu_ref[e] = jnp.dot(xt, d_up, preferred_element_type=jnp.float32).astype(jnp.bfloat16)
        gd_ref[e] = jnp.dot(dyt, gated, preferred_element_type=jnp.float32).astype(jnp.bfloat16)
        dx = lax.dot_general(d_gate, wg_ref[e], right, preferred_element_type=jnp.float32)
        dx = dx + lax.dot_general(d_up, wu_ref[e], right, preferred_element_type=jnp.float32)
        acc_ref[:, :DSH] += dx
        return 0

    lax.fori_loop(0, EXPERTS, expert, 0)
    dx_ref[:, :OUT_COLS] = acc_ref[:, :OUT_COLS].astype(jnp.bfloat16)
    dx_ref[:, OUT_COLS:] = acc_ref[:, OUT_COLS:].astype(jnp.bfloat16)


def vmem_spec():
    return pl.BlockSpec(memory_space=pltpu.VMEM)


def forward(xin, wg, wu, wd):
    return pl.pallas_call(
        forward_kernel,
        out_shape=jax.ShapeDtypeStruct((TOKENS, PACK), jnp.bfloat16),
        in_specs=[vmem_spec()] * 4,
        out_specs=vmem_spec(),
        scratch_shapes=[
            pltpu.VMEM((BLOCKS, ROWS, EXPERTS * BLK), jnp.bfloat16),
            pltpu.VMEM((BLOCKS, EXPERTS * BLK, COLS), jnp.bfloat16),
            pltpu.VMEM((TOP, TOKENS, COLS), jnp.float32),
        ],
        compiler_params=pltpu.CompilerParams(vmem_limit_bytes=VMEM),
    )(xin, wg, wu, wd)


def backward(xin, xt, pre, wg, wu):
    weight = jax.ShapeDtypeStruct((EXPERTS, DSH, FSH), jnp.bfloat16)
    return pl.pallas_call(
        backward_kernel,
        out_shape=[weight] * 3 + [jax.ShapeDtypeStruct((TOKENS, OUT_COLS + LANES), jnp.bfloat16)],
        in_specs=[vmem_spec()] * 5,
        out_specs=[vmem_spec()] * 4,
        scratch_shapes=[
            pltpu.VMEM((BLOCKS, ROWS, EXPERTS * BLK), jnp.bfloat16),
            pltpu.VMEM((BLOCKS, ROWS, COLS), jnp.bfloat16),
            pltpu.VMEM((BLOCKS, EXPERTS * BLK, COLS), jnp.bfloat16),
            pltpu.VMEM((TOKENS, OUT_COLS + LANES), jnp.float32),
        ],
        compiler_params=pltpu.CompilerParams(vmem_limit_bytes=VMEM),
    )(xin, xt, pre, wg, wu)


def exchange(value, axis):
    return lax.all_to_all(value, axis, split_axis=0, concat_axis=0, tiled=True)


def swap(value, axis):
    return lax.ppermute(value, axis, [(0, 1), (1, 0)])


def local(stash, scale_exp, grad_out, route_ids, route_probs, w_gate, w_up, w_down):
    bf16, f32 = jnp.bfloat16, jnp.float32
    factors = jnp.repeat(jnp.exp2(scale_exp.astype(f32)), DSH // scale_exp.shape[1], axis=1)
    x_local = (stash.astype(f32) * factors).astype(bf16)
    tok = stash.shape[0]
    pad = jnp.zeros((tok, COLS - PROBS_AT - TOP), bf16)
    xin = jnp.concatenate([x_local, grad_out, route_ids.astype(bf16), route_probs, pad], axis=1)
    with jax.named_scope("gather_tokens"):
        xin = lax.all_gather(xin, "zh", axis=0, tiled=True)
        xin = lax.all_gather(xin, "x", axis=0, tiled=True)
        xin = lax.all_gather(xin, "core", axis=0, tiled=True)
    wg = w_gate.reshape(EXPERTS, DSH, FSH)
    wu = w_up.reshape(EXPERTS, DSH, FSH)
    wd = w_down.reshape(EXPERTS, DSH, FSH)
    xt = xin[:, :2 * DSH].T
    pre = forward(xin, wg, wu, wd)
    with jax.named_scope("sum_pre"):
        pre = exchange(pre, "y").reshape(4, TOKENS // 4, PACK)
        pre = jnp.sum(pre.astype(f32), axis=0).astype(bf16)
        pre = exchange(pre, "zl").reshape(8, BLK, PACK)
        pre = jnp.sum(pre.astype(f32), axis=0).astype(bf16)
    with jax.named_scope("spread_pre"):
        pre = exchange(jnp.tile(pre, (8, 1)), "zl")
        pre = exchange(jnp.tile(pre, (4, 1)), "y")
    gg, gu, gd, dx = backward(xin, xt, pre, wg, wu)
    with jax.named_scope("sum_dx"):
        core = lax.axis_index("core")
        half = TOKENS // 2
        keep = lax.dynamic_slice_in_dim(dx, core * half, half, 0).astype(f32)
        give = lax.dynamic_slice_in_dim(dx, (1 - core) * half, half, 0)
        dx = (keep + swap(give, "core").astype(f32)).astype(bf16)
        dx = exchange(dx, "x").reshape(4, half // 4, dx.shape[1])
        dx = jnp.sum(dx.astype(f32), axis=0).astype(bf16)
        zh = lax.axis_index("zh")
        keep = lax.dynamic_slice_in_dim(dx, zh * tok, tok, 0).astype(f32)
        give = lax.dynamic_slice_in_dim(dx, (1 - zh) * tok, tok, 0)
        dx = keep + swap(give, "zh").astype(f32)
    grad_in = dx[:, :DSH].astype(bf16)
    grad_probs = dx[:, OUT_COLS:OUT_COLS + TOP]
    flat = w_gate.shape
    return (grad_in, grad_probs, gg.reshape(flat), gu.reshape(flat), gd.reshape(flat))


def solution(mesh):
    fine = Mesh(mesh.devices.reshape(4, 2, 2, 8, 4), DP + EX)
    in_specs = (
        P(DP, EX),
        P(DP, EX),
        P(DP, EX),
        P(DP, None),
        P(DP, None),
        P(None, DP + EX),
        P(None, DP + EX),
        P(None, DP + EX),
    )
    out_specs = (
        P(DP, EX),
        P(DP, None),
        P(None, DP + EX),
        P(None, DP + EX),
        P(None, DP + EX),
    )
    return jax.shard_map(local, mesh=fine, in_specs=in_specs, out_specs=out_specs, check_vma=False)
```

```python
import jax
import jax.numpy as jnp
from jax import lax
from jax.experimental import pallas as pl
from jax.experimental.pallas import tpu as pltpu
from jax.sharding import Mesh, PartitionSpec as P

DP = ("x", "zh", "core")
EX = ("zl", "y")
BLK = 16
TOP = 6
CAP = 8
EXPERTS = 16
DSH = 160
FSH = 96
SHARD = 32
TOKENS = 512
BLOCKS = TOKENS // BLK
LANES = 128
NG = 4
NE = EXPERTS // NG
NX = 4
SLOTS = BLOCKS * CAP
Q = DSH // 4
STEP = Q + 8
WIDE = 4 * STEP
COLS = 2 * WIDE
IDS_AT = Q
PROBS_AT = STEP + Q
TRIO = 3 * FSH
PACK = NE * TRIO
PAIR = 2 * LANES
DX_COLS = 256
VMEM = 56 * 1024 * 1024
BF16 = jnp.bfloat16
F32 = jnp.float32


def iota(shape, dim):
    return lax.broadcasted_iota(jnp.int32, shape, dim)


def dot(a, b):
    return jnp.dot(a, b, preferred_element_type=F32)


def dot_dims(a, b, left, right):
    return lax.dot_general(a, b, (((left,), (right,)), ((), ())), preferred_element_type=F32)


def feature_of(column):
    s = sum(jnp.where(column >= i * STEP, 1, 0) for i in range(1, 4))
    q = column - s * STEP
    return jnp.where((q < Q) & (column >= 0) & (column < WIDE), 4 * q + s, -1)


def ones(mask):
    return jnp.where(mask, 1.0, 0.0).astype(BF16)


def prepare_kernel(stash_ref, scale_ref, dy_ref, ids_ref, probs_ref, out_ref):
    scale = scale_ref[...]
    factor = jnp.where(scale == -2, 0.25, jnp.where(scale == -1, 0.5, jnp.where(scale == 0, 1.0, 2.0)))
    per = DSH // scale.shape[1]
    shape = (scale.shape[1], DSH)
    first = iota(shape, 0) * per
    expand = ones((iota(shape, 1) >= first) & (iota(shape, 1) < first + per))
    x = (stash_ref[...].astype(F32) * dot(factor.astype(BF16), expand)).astype(BF16)
    row, column = iota((DSH, COLS), 0), iota((DSH, COLS), 1)
    out = dot(x, ones(row == feature_of(column)))
    out = out + dot(dy_ref[...], ones(row == feature_of(column - WIDE)))
    row, column = iota((TOP, COLS), 0), iota((TOP, COLS), 1)
    out = out + dot(ids_ref[...].astype(F32).astype(BF16), ones(row == column - IDS_AT))
    out = out + dot(probs_ref[...], ones(row == column - PROBS_AT))
    out_ref[...] = out.astype(BF16)


def tokens_of(x_ref, g):
    return x_ref[:, :, g].reshape(TOKENS, COLS)


def forward_kernel(me_ref, x_ref, w_ref, pre_ref, xs_ref, ds_ref, wx_ref, gate_ref, slot_ref, pick_ref, wd_ref):
    first = me_ref[0] * NE
    head = tokens_of(x_ref, 0)[:, :LANES].astype(F32)
    ids = head[:, IDS_AT:IDS_AT + TOP]
    probs = head[:, PROBS_AT:PROBS_AT + TOP]
    lane = iota((TOKENS, LANES), 1)
    hit = jnp.zeros((TOKENS, LANES), F32)
    prob = jnp.zeros((TOKENS, LANES), F32)
    for k in range(TOP):
        same = ids[:, k:k + 1] == (lane + first).astype(F32)
        hit = jnp.where(same, 1.0, hit)
        prob = jnp.where(same, probs[:, k:k + 1], prob)
    hit = jnp.where(lane < NE, hit, 0.0)
    row, column = iota((TOKENS, TOKENS), 0), iota((TOKENS, TOKENS), 1)
    before = ones((column < row) & (column >= row - row % BLK))
    place = dot(before, hit.astype(BF16))
    block = iota((TOKENS, LANES), 0) // BLK
    slot = jnp.where(hit > 0.5, block.astype(F32) * CAP + place, -1.0)
    slot_ref[...] = slot
    slot_t = slot.T
    row = iota((SLOTS, TOKENS), 0).astype(F32)
    for e in range(NE):
        pick_ref[e * SLOTS:(e + 1) * SLOTS, :] = ones(row == slot_t[e:e + 1, :])
    pick = pick_ref[...]
    gate_ref[...] = dot(pick, prob.astype(BF16))
    for g in range(NG):
        xs_ref[g] = dot(pick, x_ref[:, :, g, :, :WIDE].reshape(TOKENS, WIDE)).astype(BF16)
        ds_ref[g] = dot(pick, x_ref[:, :, g, :, WIDE:].reshape(TOKENS, WIDE)).astype(BF16)
    low = jnp.zeros((STEP - Q, FSH), F32)
    side = jnp.zeros((STEP, LANES - FSH), F32)
    for g in range(NG):
        for e in range(NE):
            for i in range(3):
                w = w_ref[g, e, i].astype(F32)
                for s in range(4):
                    piece = jnp.concatenate([w[:, s * FSH:(s + 1) * FSH], low], axis=0)
                    piece = jnp.concatenate([piece, side], axis=1).astype(BF16)
                    if i < 2:
                        wx_ref[g, s * STEP:(s + 1) * STEP, e * PAIR + i * LANES:e * PAIR + (i + 1) * LANES] = piece
                    else:
                        wd_ref[g, s * STEP:(s + 1) * STEP, e * LANES:(e + 1) * LANES] = piece
    for e in range(NE):
        at = slice(e * SLOTS, (e + 1) * SLOTS)
        ab = jnp.zeros((SLOTS, PAIR), F32)
        back = jnp.zeros((SLOTS, LANES), F32)
        for g in range(NG):
            ab = ab + dot(xs_ref[g, at, :], wx_ref[g, :, e * PAIR:(e + 1) * PAIR])
            back = back + dot(ds_ref[g, at, :], wd_ref[g, :, e * LANES:(e + 1) * LANES])
        pieces = [ab[:, :FSH], ab[:, LANES:LANES + FSH], back[:, :FSH]]
        pre_ref[:, e * TRIO:(e + 1) * TRIO] = jnp.concatenate(pieces, axis=1).astype(BF16)


def middle_kernel(me_ref, x_ref, pre_ref, wx_ref, gate_ref, slot_ref, d_ref, dx_ref, spread_ref):
    first = me_ref[0] * NE
    side = jnp.zeros((SLOTS, LANES - FSH), F32)
    lane = iota((SLOTS, LANES - FSH), 1)
    slots = iota((TOKENS, SLOTS), 1).astype(F32)
    head = tokens_of(x_ref, 0)[:, :LANES].astype(F32)
    wide = iota((TOKENS, LANES), 1)
    tail = jnp.zeros((TOKENS, LANES), F32)
    for e in range(NE):
        pre = pre_ref[:, e * TRIO:(e + 1) * TRIO].astype(F32)
        a, b, back = (pre[:, i * FSH:(i + 1) * FSH] for i in range(3))
        gate = gate_ref[e * SLOTS:(e + 1) * SLOTS, e:e + 1]
        sig = jax.nn.sigmoid(a)
        act = a * sig
        hidden = act * b
        dh = gate * back
        d_gate = dh * b * sig * (1.0 + a * (1.0 - sig))
        prob = jnp.sum(hidden * back, axis=1, keepdims=True)
        prob = jnp.where(lane == 0, prob, 0.0)
        d = jnp.concatenate([d_gate, prob, dh * act, side, gate * hidden, side], axis=1).astype(BF16)
        d_ref[e] = d
        pick = ones(slots == slot_ref[:, e:e + 1])
        spread = dot(pick, d[:, :PAIR])
        spread_ref[:, e * PAIR:(e + 1) * PAIR] = spread.astype(BF16)
        for k in range(TOP):
            same = head[:, IDS_AT + k:IDS_AT + k + 1] == (first + e).astype(F32)
            tail = jnp.where((wide == k) & same, spread[:, FSH:FSH + 1], tail)
    tail = tail[:, :DX_COLS - WIDE]
    for g in range(NG):
        dx = dot_dims(spread_ref[...], wx_ref[g], 1, 1)
        dx = jnp.concatenate([dx, tail], axis=1).astype(BF16)
        dx_ref[:, :, g] = dx.reshape(2, NX, 2 * SHARD, DX_COLS)


def weight_kernel(xs_ref, ds_ref, d_ref, out_ref):
    for e in range(NE):
        at = slice(e * SLOTS, (e + 1) * SLOTS)
        for g in range(NG):
            both = dot_dims(xs_ref[g, at, :], d_ref[e, :, :PAIR], 0, 0)
            down = dot_dims(ds_ref[g, at, :], d_ref[e, :, PAIR:], 0, 0)
            for i, (grad, base) in enumerate(((both, 0), (both, LANES), (down, 0))):
                pieces = [grad[s * STEP:s * STEP + Q, base:base + FSH] for s in range(4)]
                out_ref[g, e, i] = jnp.concatenate(pieces, axis=1).astype(BF16)


def finish_kernel(dx_ref, got_ref, in_ref, probs_ref):
    total = dx_ref[...].astype(F32) + got_ref[...].astype(F32)
    row, column = iota((WIDE, DSH), 0), iota((WIDE, DSH), 1)
    order = ones(feature_of(row) == column)
    in_ref[...] = dot(total[:, :WIDE].astype(BF16), order).astype(BF16)
    probs_ref[...] = total[:, WIDE:WIDE + TOP]


def call(kernel, outs, args, scratch=(), scalar=False):
    vmem = pl.BlockSpec(memory_space=pltpu.VMEM)
    specs = [vmem] * len(args)
    if scalar:
        specs[0] = pl.BlockSpec(memory_space=pltpu.SMEM)
    return pl.pallas_call(
        kernel,
        out_shape=[jax.ShapeDtypeStruct(shape, dtype) for shape, dtype in outs],
        in_specs=specs,
        out_specs=[vmem] * len(outs),
        scratch_shapes=[pltpu.VMEM(shape, dtype) for shape, dtype in scratch],
        compiler_params=pltpu.CompilerParams(vmem_limit_bytes=VMEM),
    )(*args)


def exchange(value, axis):
    return lax.all_to_all(value, axis, split_axis=0, concat_axis=0, tiled=True)


def swap(value, axis):
    return lax.ppermute(value, axis, [(0, 1), (1, 0)])


def sum_first(value):
    return jnp.sum(value.astype(F32), axis=0).astype(BF16)


def local(stash, scale_exp, grad_out, route_ids, route_probs, w_gate, w_up, w_down):
    me = lax.axis_index("y").astype(jnp.int32).reshape(1)
    core = lax.axis_index("core")
    zh = lax.axis_index("zh")
    (xin,) = call(prepare_kernel, [((SHARD, COLS), BF16)], (stash, scale_exp, grad_out, route_ids, route_probs))
    with jax.named_scope("gather_tokens"):
        other = swap(xin, "zh")
        xin = jnp.where(zh == 0, jnp.concatenate([xin, other]), jnp.concatenate([other, xin]))
        xin = exchange(jnp.tile(xin, (NX * NG, 1)), ("x", "y"))
        other = swap(xin, "core")
        xin = jnp.where(core == 0, jnp.stack([xin, other]), jnp.stack([other, xin]))
        xin = xin.reshape(2, NX, NG, 2 * SHARD, COLS)
    with jax.named_scope("move_weights"):
        tiles = [w.reshape(EXPERTS, 1, Q, 4 * FSH) for w in (w_gate, w_up, w_down)]
        weights = exchange(jnp.concatenate(tiles, axis=1), "y")
        weights = weights.reshape(NG, NE, 3, Q, 4 * FSH)
    pre, xs, ds, wx, gate, slot = call(
        forward_kernel,
        [((SLOTS, PACK), BF16), ((NG, NE * SLOTS, WIDE), BF16), ((NG, NE * SLOTS, WIDE), BF16),
         ((NG, WIDE, NE * PAIR), BF16), ((NE * SLOTS, LANES), F32), ((TOKENS, LANES), F32)],
        (me, xin, weights),
        [((NE * SLOTS, TOKENS), BF16), ((NG, WIDE, NE * LANES), BF16)],
        True)
    with jax.named_scope("sum_pre"):
        pre = sum_first(exchange(pre, "zl").reshape(8, SLOTS // 8, PACK))
    with jax.named_scope("spread_pre"):
        pre = exchange(jnp.tile(pre, (8, 1)), "zl")
    d, dx = call(
        middle_kernel,
        [((NE, SLOTS, 3 * LANES), BF16), ((2, NX, NG, 2 * SHARD, DX_COLS), BF16)],
        (me, xin, pre, wx, gate, slot),
        [((TOKENS, NE * PAIR), BF16)],
        True)
    (grads,) = call(weight_kernel, [((NG, NE, 3, Q, 4 * FSH), BF16)], (xs, ds, d))
    with jax.named_scope("sum_dx"):
        keep = lax.dynamic_index_in_dim(dx, core, 0, False).astype(F32)
        give = lax.dynamic_index_in_dim(dx, 1 - core, 0, False)
        dx = (keep + swap(give, "core").astype(F32)).astype(BF16)
        dx = exchange(dx.reshape(NX * NG, 2 * SHARD, DX_COLS), ("x", "y"))
        dx = jnp.sum(dx.astype(F32), axis=0)
        keep = lax.dynamic_slice_in_dim(dx, zh * SHARD, SHARD, 0)
        give = lax.dynamic_slice_in_dim(dx, (1 - zh) * SHARD, SHARD, 0).astype(BF16)
        got = swap(give, "zh")
    with jax.named_scope("return_grads"):
        grads = exchange(grads.reshape(EXPERTS, 3, Q, 4 * FSH), "y")
        grads = [grads[:, i].reshape(w_gate.shape) for i in range(3)]
    grad_in, grad_probs = call(finish_kernel, [((SHARD, DSH), BF16), ((SHARD, TOP), F32)], (keep, got))
    return (grad_in, grad_probs, *grads)


def solution(mesh):
    fine = Mesh(mesh.devices.reshape(4, 2, 2, 8, 4), DP + EX)
    weight = P(None, DP + EX)
    in_specs = (P(DP, EX), P(DP, EX), P(DP, EX), P(DP, None), P(DP, None), weight, weight, weight)
    out_specs = (P(DP, EX), P(DP, None), weight, weight, weight)
    return jax.shard_map(local, mesh=fine, in_specs=in_specs, out_specs=out_specs, check_vma=False)
```

```python
import jax
import jax.numpy as jnp
from jax import lax
from jax.experimental import pallas as pl
from jax.experimental.pallas import tpu as pltpu
from jax.sharding import Mesh, PartitionSpec as P

DP = ("x", "zh", "core")
EX = ("zq", "zp", "y")
GROUP = ("zp", "y")
BLK = 16
TOP = 6
CAP = 8
EXPERTS = 16
DSH = 160
FSH = 96
SHARD = 32
TOKENS = 512
BLOCKS = TOKENS // BLK
LANES = 128
NG = 8
NE = EXPERTS // NG
NX = 4
SLOTS = BLOCKS * CAP
HALF = TOKENS // 2
HSLOTS = SLOTS // 2
Q = DSH // 4
STEP = Q + 8
WIDE = 4 * STEP
COLS = 2 * WIDE
IDS_AT = Q
PROBS_AT = STEP + Q
TRIO = 3 * FSH
PACK = 2 * NE * TRIO
PAIR = 2 * LANES
VMEM = 56 * 1024 * 1024
BF16 = jnp.bfloat16
F32 = jnp.float32


def iota(shape, dim):
    return lax.broadcasted_iota(jnp.int32, shape, dim)


def dot(a, b):
    return jnp.dot(a, b, preferred_element_type=F32)


def dot_dims(a, b, left, right):
    return lax.dot_general(a, b, (((left,), (right,)), ((), ())), preferred_element_type=F32)


def feature_of(column):
    s = sum(jnp.where(column >= i * STEP, 1, 0) for i in range(1, 4))
    q = column - s * STEP
    return jnp.where((q < Q) & (column >= 0) & (column < WIDE), 4 * q + s, -1)


def ones(mask):
    return jnp.where(mask, 1.0, 0.0).astype(BF16)


def prepare_kernel(stash_ref, scale_ref, dy_ref, ids_ref, probs_ref, out_ref):
    scale = scale_ref[...]
    factor = jnp.where(scale == -2, 0.25, jnp.where(scale == -1, 0.5, jnp.where(scale == 0, 1.0, 2.0)))
    per = DSH // scale.shape[0]
    shape = (scale.shape[0], DSH)
    first = iota(shape, 0) * per
    expand = ones((iota(shape, 1) >= first) & (iota(shape, 1) < first + per))
    x = (stash_ref[...].astype(F32) * dot_dims(factor.astype(BF16), expand, 0, 0)).astype(BF16)
    row, column = iota((DSH, COLS), 0), iota((DSH, COLS), 1)
    out = dot(x, ones(row == feature_of(column)))
    out = out + dot(dy_ref[...], ones(row == feature_of(column - WIDE)))
    row, column = iota((TOP, COLS), 0), iota((TOP, COLS), 1)
    out = out + dot_dims(ids_ref[...].astype(F32).astype(BF16), ones(row == column - IDS_AT), 0, 0)
    out = out + dot_dims(probs_ref[...], ones(row == column - PROBS_AT), 0, 0)
    out_ref[...] = out.astype(BF16)


def forward_kernel(me_ref, x_ref, w_ref, give_ref, keep_ref, xs_ref, ds_ref, wx_ref, gate_ref, slot_ref,
                   pick_ref, wd_ref, pre_ref):
    first = me_ref[0] * NE
    head = x_ref[:, :, 0].reshape(TOKENS, COLS)[:, :LANES].astype(F32)
    ids = head[:, IDS_AT:IDS_AT + TOP]
    probs = head[:, PROBS_AT:PROBS_AT + TOP]
    lane = iota((TOKENS, LANES), 1)
    hit = jnp.zeros((TOKENS, LANES), F32)
    prob = jnp.zeros((TOKENS, LANES), F32)
    for k in range(TOP):
        same = ids[:, k:k + 1] == (lane + first).astype(F32)
        hit = jnp.where(same, 1.0, hit)
        prob = jnp.where(same, probs[:, k:k + 1], prob)
    hit = jnp.where(lane < NE, hit, 0.0)
    row, column = iota((HALF, HALF), 0), iota((HALF, HALF), 1)
    before = ones((column < row) & (column >= row - row % BLK))
    block = (iota((HALF, LANES), 0) // BLK).astype(F32)
    row = iota((HSLOTS, HALF), 0).astype(F32)
    for h in range(2):
        at = slice(h * HALF, (h + 1) * HALF)
        place = dot(before, hit[at].astype(BF16))
        slot = jnp.where(hit[at] > 0.5, block * CAP + place, -1.0)
        slot_ref[at, :] = jnp.where(lane[at] < NE, slot, head[at])
        slot_t = slot.T
        for e in range(NE):
            pick_ref[h, e * HSLOTS:(e + 1) * HSLOTS, :] = ones(row == slot_t[e:e + 1, :])
        gate = dot(pick_ref[h], prob[at].astype(BF16))
        for e in range(NE):
            gate_ref[e, h * HSLOTS:(h + 1) * HSLOTS, :] = gate[e * HSLOTS:(e + 1) * HSLOTS]
    for g in range(NG):
        for h in range(2):
            x = dot(pick_ref[h], x_ref[h, :, g, :, :WIDE].reshape(HALF, WIDE)).astype(BF16)
            dy = dot(pick_ref[h], x_ref[h, :, g, :, WIDE:].reshape(HALF, WIDE)).astype(BF16)
            for e in range(NE):
                at = slice(h * HSLOTS, (h + 1) * HSLOTS)
                xs_ref[g, e, at, :] = x[e * HSLOTS:(e + 1) * HSLOTS]
                ds_ref[g, e, at, :] = dy[e * HSLOTS:(e + 1) * HSLOTS]
    low = jnp.zeros((STEP - Q, FSH), F32)
    side = jnp.zeros((STEP, LANES - FSH), F32)
    for g in range(NG):
        for e in range(NE):
            for i in range(3):
                w = w_ref[g, e, i].astype(F32)
                for s in range(4):
                    piece = jnp.concatenate([w[:, s * FSH:(s + 1) * FSH], low], axis=0)
                    piece = jnp.concatenate([piece, side], axis=1).astype(BF16)
                    if i < 2:
                        wx_ref[g, s * STEP:(s + 1) * STEP, e * PAIR + i * LANES:e * PAIR + (i + 1) * LANES] = piece
                    else:
                        wd_ref[g, s * STEP:(s + 1) * STEP, e * LANES:(e + 1) * LANES] = piece
    for e in range(NE):
        ab = jnp.zeros((SLOTS, PAIR), F32)
        back = jnp.zeros((SLOTS, LANES), F32)
        for g in range(NG):
            ab = ab + dot(xs_ref[g, e], wx_ref[g, :, e * PAIR:(e + 1) * PAIR])
            back = back + dot(ds_ref[g, e], wd_ref[g, :, e * LANES:(e + 1) * LANES])
        trio = jnp.concatenate([ab[:, :FSH], ab[:, LANES:LANES + FSH], back[:, :FSH]], axis=1)
        for h in range(2):
            unit = 2 * e + h
            pre_ref[:, unit * TRIO:(unit + 1) * TRIO] = trio[h * HSLOTS:(h + 1) * HSLOTS]
    bit, half = me_ref[1], HSLOTS // 2
    keep_ref[...] = pre_ref[pl.ds(pl.multiple_of(bit * half, half), half), :]
    give_ref[...] = pre_ref[pl.ds(pl.multiple_of((1 - bit) * half, half), half), :].astype(BF16)


def middle_kernel(me_ref, pre_ref, wx_ref, gate_ref, slot_ref, d_ref, keep_ref, give_ref, spread_ref, tail_ref):
    first = me_ref[0] * NE
    side = jnp.zeros((HSLOTS, LANES - FSH), F32)
    lane = iota((HSLOTS, LANES - FSH), 1)
    slots = iota((HALF, HSLOTS), 1).astype(F32)
    wide = iota((HALF, LANES), 1)
    for h in range(2):
        info = slot_ref[h * HALF:(h + 1) * HALF, :]
        tail = jnp.zeros((HALF, LANES), F32)
        for e in range(NE):
            base = (2 * e + h) * TRIO
            pre = pre_ref[:, base:base + TRIO].astype(F32)
            a, b, back = (pre[:, i * FSH:(i + 1) * FSH] for i in range(3))
            gate = gate_ref[e, h * HSLOTS:(h + 1) * HSLOTS, e:e + 1]
            sig = jax.nn.sigmoid(a)
            act = a * sig
            hidden = act * b
            dh = gate * back
            d_gate = dh * b * sig * (1.0 + a * (1.0 - sig))
            prob = jnp.sum(hidden * back, axis=1, keepdims=True)
            prob = jnp.where(lane == 0, prob, 0.0)
            d = jnp.concatenate([d_gate, prob, dh * act, side, gate * hidden, side], axis=1).astype(BF16)
            d_ref[e, h * HSLOTS:(h + 1) * HSLOTS, :] = d
            spread = dot(ones(slots == info[:, e:e + 1]), d[:, :PAIR])
            spread_ref[h, :, e * PAIR:(e + 1) * PAIR] = spread.astype(BF16)
            mine = info == (first + e).astype(F32)
            mine = mine & (wide >= IDS_AT) & (wide < IDS_AT + TOP)
            tail = jnp.where(mine, spread[:, FSH:FSH + 1], tail)
        tail_ref[h] = tail
    none = jnp.zeros((HALF, WIDE - LANES), F32)
    for out_ref, h in ((keep_ref, me_ref[1]), (give_ref, 1 - me_ref[1])):
        tail = jnp.concatenate([tail_ref[h], none], axis=1)
        for g in range(NG):
            dx = dot_dims(spread_ref[h], wx_ref[g], 1, 1) + tail
            dx = dx.reshape(NX, 2, SHARD, WIDE)
            dx = jnp.concatenate([dx[:, 0], dx[:, 1]], axis=2)
            out_ref[:, g] = dx.astype(BF16)


def weight_kernel(xs_ref, ds_ref, d_ref, out_ref):
    for e in range(NE):
        for g in range(NG):
            both = dot_dims(xs_ref[g, e], d_ref[e, :, :PAIR], 0, 0)
            down = dot_dims(ds_ref[g, e], d_ref[e, :, PAIR:], 0, 0)
            for i, (grad, base) in enumerate(((both, 0), (both, LANES), (down, 0))):
                pieces = [grad[s * STEP:s * STEP + Q, base:base + FSH] for s in range(4)]
                out_ref[g, e, i] = jnp.concatenate(pieces, axis=1).astype(BF16)


def finish_kernel(dx_ref, got_ref, in_ref, probs_ref):
    total = dx_ref[...] + got_ref[...].astype(F32)
    row, column = iota((WIDE, DSH), 0), iota((WIDE, DSH), 1)
    order = ones(feature_of(row) == column)
    in_ref[...] = dot(total.astype(BF16), order).astype(BF16)
    probs_ref[...] = total[:, IDS_AT:IDS_AT + TOP]


def call(kernel, outs, args, scratch=(), scalar=False):
    vmem = pl.BlockSpec(memory_space=pltpu.VMEM)
    specs = [vmem] * len(args)
    if scalar:
        specs[0] = pl.BlockSpec(memory_space=pltpu.SMEM)
    return pl.pallas_call(
        kernel,
        out_shape=[jax.ShapeDtypeStruct(shape, dtype) for shape, dtype in outs],
        in_specs=specs,
        out_specs=[vmem] * len(outs),
        scratch_shapes=[pltpu.VMEM(shape, dtype) for shape, dtype in scratch],
        compiler_params=pltpu.CompilerParams(vmem_limit_bytes=VMEM),
    )(*args)


def exchange(value, axis):
    return lax.all_to_all(value, axis, split_axis=0, concat_axis=0, tiled=True)


def swap(value, axis):
    return lax.ppermute(value, axis, [(0, 1), (1, 0)])


def flip(value, axis, bit):
    return lax.ppermute(value, axis, [(i, i ^ bit) for i in range(lax.axis_size(axis))])


def local(stash, scale_exp, grad_out, route_ids, route_probs, w_gate, w_up, w_down):
    group = lax.axis_index(GROUP).astype(jnp.int32)
    core = lax.axis_index("core").astype(jnp.int32)
    zh = lax.axis_index("zh")
    zq = lax.axis_index("zq").astype(jnp.int32)
    near, far = zq % 2, zq // 2
    small = [v.T for v in (scale_exp, route_ids, route_probs)]
    (xin,) = call(prepare_kernel, [((SHARD, COLS), BF16)], (stash, small[0], grad_out, small[1], small[2]))
    other = swap(xin, "zh")
    with jax.named_scope("move_weights"):
        tiles = [w.reshape(EXPERTS, 1, Q, 4 * FSH) for w in (w_gate, w_up, w_down)]
        weights = exchange(jnp.concatenate(tiles, axis=1), GROUP)
        weights = weights.reshape(NG, NE, 3, Q, 4 * FSH)
    other, weights = lax.optimization_barrier((other, weights))
    with jax.named_scope("gather_tokens"):
        xin = jnp.where(zh == 0, jnp.concatenate([xin, other]), jnp.concatenate([other, xin]))
        xin = exchange(jnp.tile(xin, (NX * NG, 1)), ("x",) + GROUP)
        other = swap(xin, "core")
        xin = jnp.where(core == 0, jnp.stack([xin, other]), jnp.stack([other, xin]))
        xin = xin.reshape(2, NX, NG, 2 * SHARD, COLS)
    give, keep, xs, ds, wx, gate, slot = call(
        forward_kernel,
        [((HSLOTS // 2, PACK), BF16), ((HSLOTS // 2, PACK), F32), ((NG, NE, SLOTS, WIDE), BF16),
         ((NG, NE, SLOTS, WIDE), BF16), ((NG, WIDE, NE * PAIR), BF16), ((NE, SLOTS, LANES), F32),
         ((TOKENS, LANES), F32)],
        (jnp.stack([group, near]), xin, weights),
        [((2, HALF, HALF), BF16), ((NG, WIDE, NE * LANES), BF16), ((HSLOTS, PACK), F32)],
        True)
    rows = HSLOTS // 4
    with jax.named_scope("sum_pre"):
        pre = keep + flip(give, "zq", 1).astype(F32)
        keep = lax.dynamic_slice_in_dim(pre, far * rows, rows, 0)
        give = lax.dynamic_slice_in_dim(pre, (1 - far) * rows, rows, 0).astype(BF16)
        pre = (keep + flip(give, "zq", 2).astype(F32)).astype(BF16)
    with jax.named_scope("spread_pre"):
        other = flip(pre, "zq", 2)
        pre = jnp.where(far == 0, jnp.concatenate([pre, other]), jnp.concatenate([other, pre]))
        other = flip(pre, "zq", 1)
        pre = jnp.where(near == 0, jnp.concatenate([pre, other]), jnp.concatenate([other, pre]))
    d, keep, give = call(
        middle_kernel,
        [((NE, SLOTS, 3 * LANES), BF16), ((NX, NG, SHARD, COLS), BF16), ((NX, NG, SHARD, COLS), BF16)],
        (jnp.stack([group, core]), pre, wx, gate, slot),
        [((2, HALF, NE * PAIR), BF16), ((2, HALF, LANES), F32)],
        True)
    (grads,) = call(weight_kernel, [((NG, NE, 3, Q, 4 * FSH), BF16)], (xs, ds, d))
    with jax.named_scope("sum_dx"):
        dx = (keep.astype(F32) + swap(give, "core").astype(F32)).astype(BF16)
        dx = exchange(dx.reshape(NX * NG, SHARD, COLS), ("x",) + GROUP)
        dx = jnp.sum(dx.astype(F32), axis=0)
        low, high = dx[:, :WIDE], dx[:, WIDE:]
        got = swap(jnp.where(zh == 0, high, low).astype(BF16), "zh")
        keep = jnp.where(zh == 0, low, high)
    with jax.named_scope("return_grads"):
        grads = exchange(grads.reshape(EXPERTS, 3, Q, 4 * FSH), GROUP)
        grads = [grads[:, i].reshape(w_gate.shape) for i in range(3)]
    grad_in, grad_probs = call(finish_kernel, [((SHARD, DSH), BF16), ((SHARD, TOP), F32)], (keep, got))
    return (grad_in, grad_probs, *grads)


def solution(mesh):
    fine = Mesh(mesh.devices.reshape(4, 2, 2, 4, 2, 4), DP + EX)
    weight = P(None, DP + EX)
    in_specs = (P(DP, EX), P(DP, EX), P(DP, EX), P(DP, None), P(DP, None), weight, weight, weight)
    out_specs = (P(DP, EX), P(DP, None), weight, weight, weight)
    return jax.shard_map(local, mesh=fine, in_specs=in_specs, out_specs=out_specs, check_vma=False)
```

```python
import jax
import jax.numpy as jnp
from jax import lax
from jax.experimental import pallas as pl
from jax.experimental.pallas import tpu as pltpu
from jax.sharding import Mesh, PartitionSpec as P

DP = ("x", "zh", "core")
EX = ("zq", "zp", "y")
GROUP = ("zp", "y")
BLK = 16
TOP = 6
CAP = 8
EXPERTS = 16
DSH = 160
FSH = 96
SHARD = 32
TOKENS = 512
BLOCKS = TOKENS // BLK
LANES = 128
NG = 8
NE = EXPERTS // NG
NX = 4
SLOTS = BLOCKS * CAP
HALF = TOKENS // 2
HSLOTS = SLOTS // 2
PART = HSLOTS // 4
Q = DSH // 4
STEP = Q + 8
WIDE = 4 * STEP
COLS = 2 * WIDE
IDS_AT = Q
PROBS_AT = STEP + Q
TRIO = 3 * FSH
PACK = 2 * NE * TRIO
PAIR = 2 * LANES
VMEM = 56 * 1024 * 1024
BF16 = jnp.bfloat16
F32 = jnp.float32


def iota(shape, dim):
    return lax.broadcasted_iota(jnp.int32, shape, dim)


def dot(a, b):
    return jnp.dot(a, b, preferred_element_type=F32)


def dot_dims(a, b, left, right):
    return lax.dot_general(a, b, (((left,), (right,)), ((), ())), preferred_element_type=F32)


def feature_of(column):
    s = sum(jnp.where(column >= i * STEP, 1, 0) for i in range(1, 4))
    q = column - s * STEP
    return jnp.where((q < Q) & (column >= 0) & (column < WIDE), 4 * q + s, -1)


def ones(mask):
    return jnp.where(mask, 1.0, 0.0).astype(BF16)


def prepare_kernel(stash_ref, scale_ref, dy_ref, ids_ref, probs_ref, out_ref):
    scale = scale_ref[...]
    factor = jnp.where(scale == -2, 0.25, jnp.where(scale == -1, 0.5, jnp.where(scale == 0, 1.0, 2.0)))
    per = DSH // scale.shape[0]
    shape = (scale.shape[0], DSH)
    first = iota(shape, 0) * per
    expand = ones((iota(shape, 1) >= first) & (iota(shape, 1) < first + per))
    x = (stash_ref[...].astype(F32) * dot_dims(factor.astype(BF16), expand, 0, 0)).astype(BF16)
    row, column = iota((DSH, COLS), 0), iota((DSH, COLS), 1)
    out = dot(x, ones(row == feature_of(column)))
    out = out + dot(dy_ref[...], ones(row == feature_of(column - WIDE)))
    row, column = iota((TOP, COLS), 0), iota((TOP, COLS), 1)
    out = out + dot_dims(ids_ref[...].astype(F32).astype(BF16), ones(row == column - IDS_AT), 0, 0)
    out = out + dot_dims(probs_ref[...], ones(row == column - PROBS_AT), 0, 0)
    out_ref[...] = out.astype(BF16)


def layout_kernel(w_ref, wx_ref, wd_ref):
    low = jnp.zeros((STEP - Q, FSH), F32)
    side = jnp.zeros((STEP, LANES - FSH), F32)
    for g in range(NG):
        for e in range(NE):
            for i in range(3):
                w = w_ref[g, e, i].astype(F32)
                for s in range(4):
                    piece = jnp.concatenate([w[:, s * FSH:(s + 1) * FSH], low], axis=0)
                    piece = jnp.concatenate([piece, side], axis=1).astype(BF16)
                    if i < 2:
                        wx_ref[g, s * STEP:(s + 1) * STEP, e * PAIR + i * LANES:e * PAIR + (i + 1) * LANES] = piece
                    else:
                        wd_ref[g, s * STEP:(s + 1) * STEP, e * LANES:(e + 1) * LANES] = piece


def forward_kernel(me_ref, x0_ref, x1_ref, wx_ref, wd_ref, keep_ref, give1_ref, give2_ref, give3_ref,
                   xs_ref, ds_ref, gate_ref, slot_ref, pick_ref, pre_ref):
    first = me_ref[0] * NE
    lane = iota((HALF, LANES), 1)
    row, column = iota((HALF, HALF), 0), iota((HALF, HALF), 1)
    before = ones((column < row) & (column >= row - row % BLK))
    block = (iota((HALF, LANES), 0) // BLK).astype(F32)
    row = iota((HSLOTS, HALF), 0).astype(F32)
    for h, x_ref in enumerate((x0_ref, x1_ref)):
        at = slice(h * HALF, (h + 1) * HALF)
        head = x_ref[:, 0, :, :LANES].reshape(HALF, LANES).astype(F32)
        hit = jnp.zeros((HALF, LANES), F32)
        prob = jnp.zeros((HALF, LANES), F32)
        for k in range(TOP):
            same = head[:, IDS_AT + k:IDS_AT + k + 1] == (lane + first).astype(F32)
            hit = jnp.where(same, 1.0, hit)
            prob = jnp.where(same, head[:, PROBS_AT + k:PROBS_AT + k + 1], prob)
        place = dot(before, hit.astype(BF16))
        slot = jnp.where(hit > 0.5, block * CAP + place, -1.0)
        slot_ref[at, :] = jnp.where(lane < NE, slot, head)
        slot_t = slot.T
        for e in range(NE):
            pick_ref[h, e * HSLOTS:(e + 1) * HSLOTS, :] = ones(row == slot_t[e:e + 1, :])
        gate = dot(pick_ref[h], prob.astype(BF16))
        for e in range(NE):
            gate_ref[e, h * HSLOTS:(h + 1) * HSLOTS, :] = gate[e * HSLOTS:(e + 1) * HSLOTS]
    for g in range(NG):
        for h, x_ref in enumerate((x0_ref, x1_ref)):
            x = dot(pick_ref[h], x_ref[:, g, :, :WIDE].reshape(HALF, WIDE)).astype(BF16)
            dy = dot(pick_ref[h], x_ref[:, g, :, WIDE:].reshape(HALF, WIDE)).astype(BF16)
            at = slice(h * HSLOTS, (h + 1) * HSLOTS)
            for e in range(NE):
                xs_ref[g, e, at, :] = x[e * HSLOTS:(e + 1) * HSLOTS]
                ds_ref[g, e, at, :] = dy[e * HSLOTS:(e + 1) * HSLOTS]
    for e in range(NE):
        ab = jnp.zeros((SLOTS, PAIR), F32)
        back = jnp.zeros((SLOTS, LANES), F32)
        for g in range(NG):
            ab = ab + dot(xs_ref[g, e], wx_ref[g, :, e * PAIR:(e + 1) * PAIR])
            back = back + dot(ds_ref[g, e], wd_ref[g, :, e * LANES:(e + 1) * LANES])
        trio = jnp.concatenate([ab[:, :FSH], ab[:, LANES:LANES + FSH], back[:, :FSH]], axis=1)
        for h in range(2):
            unit = 2 * e + h
            pre_ref[:, unit * TRIO:(unit + 1) * TRIO] = trio[h * HSLOTS:(h + 1) * HSLOTS]
    for s, out_ref in enumerate((keep_ref, give1_ref, give2_ref, give3_ref)):
        rows = pl.ds(pl.multiple_of(me_ref[1 + s] * PART, PART), PART)
        out_ref[...] = pre_ref[rows, :].astype(out_ref.dtype)


def dx_of(spread, wx, tail):
    dx = dot_dims(spread, wx, 1, 1) + tail
    dx = dx.reshape(NX, 2, SHARD, WIDE)
    return jnp.concatenate([dx[:, 0], dx[:, 1]], axis=2)


def middle_kernel(me_ref, own_ref, pre1_ref, pre2_ref, pre3_ref, wx_ref, gate_ref, slot_ref,
                  d_ref, spread_ref, tail_ref, give_ref, pre_ref, far_ref):
    first = me_ref[0] * NE
    for s, part_ref in enumerate((own_ref, pre1_ref, pre2_ref, pre3_ref)):
        rows = pl.ds(pl.multiple_of(me_ref[1 + s] * PART, PART), PART)
        pre_ref[rows, :] = part_ref[...].astype(F32)
    side = jnp.zeros((HSLOTS, LANES - FSH), F32)
    lane = iota((HSLOTS, LANES - FSH), 1)
    slots = iota((HALF, HSLOTS), 1).astype(F32)
    wide = iota((HALF, LANES), 1)
    none = jnp.zeros((HALF, WIDE - LANES), F32)
    for h, out_ref in enumerate((spread_ref, far_ref)):
        info = slot_ref[h * HALF:(h + 1) * HALF, :]
        tail = jnp.zeros((HALF, LANES), F32)
        for e in range(NE):
            base = (2 * e + h) * TRIO
            pre = pre_ref[:, base:base + TRIO]
            a, b, back = (pre[:, i * FSH:(i + 1) * FSH] for i in range(3))
            gate = gate_ref[e, h * HSLOTS:(h + 1) * HSLOTS, e:e + 1]
            sig = jax.nn.sigmoid(a)
            act = a * sig
            hidden = act * b
            dh = gate * back
            d_gate = dh * b * sig * (1.0 + a * (1.0 - sig))
            prob = jnp.sum(hidden * back, axis=1, keepdims=True)
            prob = jnp.where(lane == 0, prob, 0.0)
            d = jnp.concatenate([d_gate, prob, dh * act, side, gate * hidden, side], axis=1).astype(BF16)
            d_ref[e, h * HSLOTS:(h + 1) * HSLOTS, :] = d
            spread = dot(ones(slots == info[:, e:e + 1]), d[:, :PAIR])
            out_ref[:, e * PAIR:(e + 1) * PAIR] = spread.astype(BF16)
            mine = info == (first + e).astype(F32)
            mine = mine & (wide >= IDS_AT) & (wide < IDS_AT + TOP)
            tail = jnp.where(mine, spread[:, FSH:FSH + 1], tail)
        if h == 0:
            tail_ref[...] = tail
    tail = jnp.concatenate([tail, none], axis=1)
    for g in range(NG):
        give_ref[:, g] = dx_of(far_ref[...], wx_ref[g], tail).astype(BF16)


def input_kernel(got_ref, spread_ref, tail_ref, wx_ref, dx_ref):
    none = jnp.zeros((HALF, WIDE - LANES), F32)
    tail = jnp.concatenate([tail_ref[...], none], axis=1)
    for g in range(NG):
        dx = dx_of(spread_ref[...], wx_ref[g], tail) + got_ref[:, g].astype(F32)
        dx_ref[:, g] = dx.astype(BF16)


def weight_kernel(xs_ref, ds_ref, d_ref, out_ref):
    for e in range(NE):
        for g in range(NG):
            both = dot_dims(xs_ref[g, e], d_ref[e, :, :PAIR], 0, 0)
            down = dot_dims(ds_ref[g, e], d_ref[e, :, PAIR:], 0, 0)
            for i, (grad, base) in enumerate(((both, 0), (both, LANES), (down, 0))):
                pieces = [grad[s * STEP:s * STEP + Q, base:base + FSH] for s in range(4)]
                out_ref[g, e, i] = jnp.concatenate(pieces, axis=1).astype(BF16)


def finish_kernel(dx_ref, got_ref, in_ref, probs_ref):
    total = dx_ref[...] + got_ref[...].astype(F32)
    row, column = iota((WIDE, DSH), 0), iota((WIDE, DSH), 1)
    order = ones(feature_of(row) == column)
    in_ref[...] = dot(total.astype(BF16), order).astype(BF16)
    probs_ref[...] = total[:, :LANES].T[IDS_AT:IDS_AT + TOP, :]


def call(kernel, outs, args, scratch=(), scalar=False):
    vmem = pl.BlockSpec(memory_space=pltpu.VMEM)
    specs = [vmem] * len(args)
    if scalar:
        specs[0] = pl.BlockSpec(memory_space=pltpu.SMEM)
    return pl.pallas_call(
        kernel,
        out_shape=[jax.ShapeDtypeStruct(shape, dtype) for shape, dtype in outs],
        in_specs=specs,
        out_specs=[vmem] * len(outs),
        scratch_shapes=[pltpu.VMEM(shape, dtype) for shape, dtype in scratch],
        compiler_params=pltpu.CompilerParams(vmem_limit_bytes=VMEM),
    )(*args)


def exchange(value, axis):
    return lax.all_to_all(value, axis, split_axis=0, concat_axis=0, tiled=True)


def swap(value, axis):
    return lax.ppermute(value, axis, [(0, 1), (1, 0)])


def flip(value, axis, bit):
    return lax.ppermute(value, axis, [(i, i ^ bit) for i in range(lax.axis_size(axis))])


def local(stash, scale_exp, grad_out, route_ids, route_probs, w_gate, w_up, w_down):
    group = lax.axis_index(GROUP).astype(jnp.int32)
    zq = lax.axis_index("zq").astype(jnp.int32)
    me = jnp.stack([group] + [zq ^ s for s in range(4)])
    small = [v.T for v in (scale_exp, route_ids, route_probs)]
    (xin,) = call(prepare_kernel, [((SHARD, COLS), BF16)], (stash, small[0], grad_out, small[1], small[2]))
    other = swap(xin, "zh")
    with jax.named_scope("move_weights"):
        xin, w_gate, w_up, w_down = lax.optimization_barrier((xin, w_gate, w_up, w_down))
        tiles = [w.reshape(EXPERTS, 1, Q, 4 * FSH) for w in (w_gate, w_up, w_down)]
        weights = exchange(jnp.concatenate(tiles, axis=1), GROUP)
        weights = weights.reshape(NG, NE, 3, Q, 4 * FSH)
    other, weights = lax.optimization_barrier((other, weights))
    with jax.named_scope("gather_tokens"):
        xin = jnp.tile(jnp.concatenate([xin, other]), (NX * NG, 1))
        x0 = exchange(xin, ("x",) + GROUP).reshape(NX, NG, 2 * SHARD, COLS)
        x1 = swap(x0, "core")
    wx, wd = call(layout_kernel, [((NG, WIDE, NE * PAIR), BF16), ((NG, WIDE, NE * LANES), BF16)], (weights,))
    part = ((PART, PACK), BF16)
    keep, give1, give2, give3, xs, ds, gate, slot = call(
        forward_kernel,
        [((PART, PACK), F32), part, part, part, ((NG, NE, SLOTS, WIDE), BF16), ((NG, NE, SLOTS, WIDE), BF16),
         ((NE, SLOTS, LANES), F32), ((TOKENS, LANES), F32)],
        (me, x0, x1, wx, wd),
        [((2, HALF, HALF), BF16), ((HSLOTS, PACK), F32)],
        True)
    with jax.named_scope("sum_pre"):
        got = [flip(give, "zq", 1 + i) for i, give in enumerate((give1, give2, give3))]
        pre = (keep + sum(v.astype(F32) for v in got)).astype(BF16)
    with jax.named_scope("spread_pre"):
        pre = [pre] + [flip(pre, "zq", s) for s in range(1, 4)]
    dx_shape = (NX, NG, SHARD, COLS)
    d, spread, tail, give = call(
        middle_kernel,
        [((NE, SLOTS, 3 * LANES), BF16), ((HALF, NE * PAIR), BF16), ((HALF, LANES), F32), (dx_shape, BF16)],
        (me, *pre, wx, gate, slot),
        [((HSLOTS, PACK), F32), ((HALF, NE * PAIR), BF16)],
        True)
    with jax.named_scope("sum_dx"):
        (dx,) = call(input_kernel, [(dx_shape, BF16)], (swap(give, "core"), spread, tail, wx))
        dx, d = lax.optimization_barrier((dx, d))
        dx = exchange(dx.reshape(NX * NG, SHARD, COLS), ("x",) + GROUP)
        dx = jnp.sum(dx.astype(F32), axis=0)
        keep, give = dx[:, :WIDE], dx[:, WIDE:].astype(BF16)
    (grads,) = call(weight_kernel, [((NG, NE, 3, Q, 4 * FSH), BF16)], (xs, ds, d))
    give, grads = lax.optimization_barrier((give, grads))
    got = swap(give, "zh")
    with jax.named_scope("return_grads"):
        grads = exchange(grads.reshape(EXPERTS, 3, Q, 4 * FSH), GROUP)
        grads = [grads[:, i].reshape(w_gate.shape) for i in range(3)]
    keep, *grads = lax.optimization_barrier((keep, *grads))
    grad_in, grad_probs = call(finish_kernel, [((SHARD, DSH), BF16), ((TOP, SHARD), F32)], (keep, got))
    return (grad_in, grad_probs.T, *grads)


def solution(mesh):
    fine = Mesh(mesh.devices.reshape(4, 2, 2, 4, 2, 4), DP + EX)
    weight = P(None, DP + EX)
    in_specs = (P(DP, EX), P(DP, EX), P(DP, EX), P(DP, None), P(DP, None), weight, weight, weight)
    out_specs = (P(DP, EX), P(DP, None), weight, weight, weight)
    return jax.shard_map(local, mesh=fine, in_specs=in_specs, out_specs=out_specs, check_vma=False)
```

```python
import jax
import jax.numpy as jnp
from jax import lax
from jax.experimental import pallas as pl
from jax.experimental.pallas import tpu as pltpu
from jax.sharding import Mesh, PartitionSpec as P

DP = ("x", "zh", "core")
EX = ("zq", "zp", "y")
GROUP = ("zp", "y")
BLK = 16
TOP = 6
CAP = 8
EXPERTS = 16
DSH = 160
FSH = 96
SHARD = 32
TOKENS = 512
BLOCKS = TOKENS // BLK
LANES = 128
NG = 8
NE = EXPERTS // NG
NX = 4
SLOTS = BLOCKS * CAP
HALF = TOKENS // 2
HSLOTS = SLOTS // 2
PART = HSLOTS // 4
Q = DSH // 4
STEP = Q + 8
WIDE = 4 * STEP
COLS = 2 * WIDE
IDS_AT = Q
PROBS_AT = STEP + Q
TRIO = 3 * FSH
PACK = 2 * NE * TRIO
PAIR = 2 * LANES
VMEM = 56 * 1024 * 1024
BF16 = jnp.bfloat16
F32 = jnp.float32


def iota(shape, dim):
    return lax.broadcasted_iota(jnp.int32, shape, dim)


def dot(a, b):
    return jnp.dot(a, b, preferred_element_type=F32)


def dot_dims(a, b, left, right):
    return lax.dot_general(a, b, (((left,), (right,)), ((), ())), preferred_element_type=F32)


def feature_of(column):
    s = sum(jnp.where(column >= i * STEP, 1, 0) for i in range(1, 4))
    q = column - s * STEP
    return jnp.where((q < Q) & (column >= 0) & (column < WIDE), 4 * q + s, -1)


def ones(mask):
    return jnp.where(mask, 1.0, 0.0).astype(BF16)


def prepare_kernel(stash_ref, scale_ref, dy_ref, ids_ref, probs_ref, out_ref):
    scale = scale_ref[...]
    factor = jnp.where(scale == -2, 0.25, jnp.where(scale == -1, 0.5, jnp.where(scale == 0, 1.0, 2.0)))
    per = DSH // scale.shape[0]
    shape = (scale.shape[0], DSH)
    first = iota(shape, 0) * per
    expand = ones((iota(shape, 1) >= first) & (iota(shape, 1) < first + per))
    x = (stash_ref[...].astype(F32) * dot_dims(factor.astype(BF16), expand, 0, 0)).astype(BF16)
    row, column = iota((DSH, COLS), 0), iota((DSH, COLS), 1)
    out = dot(x, ones(row == feature_of(column)))
    out = out + dot(dy_ref[...], ones(row == feature_of(column - WIDE)))
    row, column = iota((TOP, COLS), 0), iota((TOP, COLS), 1)
    out = out + dot_dims(ids_ref[...].astype(F32).astype(BF16), ones(row == column - IDS_AT), 0, 0)
    out = out + dot_dims(probs_ref[...], ones(row == column - PROBS_AT), 0, 0)
    out_ref[...] = out.astype(BF16)


def select_kernel(me_ref, a0_ref, b0_ref, a1_ref, b1_ref, xs_ref, ds_ref, gate_ref, slot_ref, pick_ref):
    first = me_ref[0] * NE
    lane = iota((HALF, LANES), 1)
    row, column = iota((HALF, HALF), 0), iota((HALF, HALF), 1)
    before = ones((column < row) & (column >= row - row % BLK))
    block = (iota((HALF, LANES), 0) // BLK).astype(F32)
    row = iota((HSLOTS, HALF), 0).astype(F32)
    pairs = ((a0_ref, b0_ref), (a1_ref, b1_ref))

    def tokens(pair, g, lanes):
        rows = HALF // 2
        return jnp.concatenate([ref[:, g, :, lanes].reshape(rows, lanes.stop - lanes.start) for ref in pair], axis=0)

    for h, pair in enumerate(pairs):
        at = slice(h * HALF, (h + 1) * HALF)
        head = tokens(pair, 0, slice(0, LANES)).astype(F32)
        hit = jnp.zeros((HALF, LANES), F32)
        prob = jnp.zeros((HALF, LANES), F32)
        for k in range(TOP):
            same = head[:, IDS_AT + k:IDS_AT + k + 1] == (lane + first).astype(F32)
            hit = jnp.where(same, 1.0, hit)
            prob = jnp.where(same, head[:, PROBS_AT + k:PROBS_AT + k + 1], prob)
        place = dot(before, hit.astype(BF16))
        slot = jnp.where(hit > 0.5, block * CAP + place, -1.0)
        slot_ref[at, :] = jnp.where(lane < NE, slot, head)
        slot_t = slot.T
        for e in range(NE):
            pick_ref[h, e * HSLOTS:(e + 1) * HSLOTS, :] = ones(row == slot_t[e:e + 1, :])
        gate = dot(pick_ref[h], prob.astype(BF16))
        for e in range(NE):
            gate_ref[e, h * HSLOTS:(h + 1) * HSLOTS, :] = gate[e * HSLOTS:(e + 1) * HSLOTS]
    for g in range(NG):
        for h, pair in enumerate(pairs):
            x = dot(pick_ref[h], tokens(pair, g, slice(0, WIDE))).astype(BF16)
            dy = dot(pick_ref[h], tokens(pair, g, slice(WIDE, COLS))).astype(BF16)
            at = slice(h * HSLOTS, (h + 1) * HSLOTS)
            for e in range(NE):
                xs_ref[g, e, at, :] = x[e * HSLOTS:(e + 1) * HSLOTS]
                ds_ref[g, e, at, :] = dy[e * HSLOTS:(e + 1) * HSLOTS]


def forward_kernel(me_ref, w_ref, xs_ref, ds_ref, keep_ref, give1_ref, give2_ref, give3_ref, wx_ref, wd_ref, pre_ref):
    low = jnp.zeros((STEP - Q, FSH), F32)
    side = jnp.zeros((STEP, LANES - FSH), F32)
    for g in range(NG):
        for e in range(NE):
            for i in range(3):
                w = w_ref[g, e, i].astype(F32)
                for s in range(4):
                    piece = jnp.concatenate([w[:, s * FSH:(s + 1) * FSH], low], axis=0)
                    piece = jnp.concatenate([piece, side], axis=1).astype(BF16)
                    if i < 2:
                        wx_ref[g, s * STEP:(s + 1) * STEP, e * PAIR + i * LANES:e * PAIR + (i + 1) * LANES] = piece
                    else:
                        wd_ref[g, s * STEP:(s + 1) * STEP, e * LANES:(e + 1) * LANES] = piece
    for e in range(NE):
        ab = jnp.zeros((SLOTS, PAIR), F32)
        back = jnp.zeros((SLOTS, LANES), F32)
        for g in range(NG):
            ab = ab + dot(xs_ref[g, e], wx_ref[g, :, e * PAIR:(e + 1) * PAIR])
            back = back + dot(ds_ref[g, e], wd_ref[g, :, e * LANES:(e + 1) * LANES])
        trio = jnp.concatenate([ab[:, :FSH], ab[:, LANES:LANES + FSH], back[:, :FSH]], axis=1)
        for h in range(2):
            unit = 2 * e + h
            pre_ref[:, unit * TRIO:(unit + 1) * TRIO] = trio[h * HSLOTS:(h + 1) * HSLOTS]
    for s, out_ref in enumerate((keep_ref, give1_ref, give2_ref, give3_ref)):
        rows = pl.ds(pl.multiple_of(me_ref[1 + s] * PART, PART), PART)
        out_ref[...] = pre_ref[rows, :].astype(out_ref.dtype)


def dx_of(spread, wx, tail):
    dx = dot_dims(spread, wx, 1, 1) + tail
    return jnp.concatenate([dx[:HALF // 2], dx[HALF // 2:]], axis=1).reshape(NX, SHARD, COLS)


def middle_kernel(me_ref, own_ref, pre1_ref, pre2_ref, pre3_ref, wx_ref, gate_ref, slot_ref,
                  d_ref, spread_ref, tail_ref, give_ref, pre_ref, far_ref):
    first = me_ref[0] * NE
    for s, part_ref in enumerate((own_ref, pre1_ref, pre2_ref, pre3_ref)):
        rows = pl.ds(pl.multiple_of(me_ref[1 + s] * PART, PART), PART)
        pre_ref[rows, :] = part_ref[...].astype(F32)
    side = jnp.zeros((HSLOTS, LANES - FSH), F32)
    lane = iota((HSLOTS, LANES - FSH), 1)
    slots = iota((HALF, HSLOTS), 1).astype(F32)
    wide = iota((HALF, LANES), 1)
    none = jnp.zeros((HALF, WIDE - LANES), F32)
    for h, out_ref in enumerate((spread_ref, far_ref)):
        info = slot_ref[h * HALF:(h + 1) * HALF, :]
        tail = jnp.zeros((HALF, LANES), F32)
        for e in range(NE):
            base = (2 * e + h) * TRIO
            pre = pre_ref[:, base:base + TRIO]
            a, b, back = (pre[:, i * FSH:(i + 1) * FSH] for i in range(3))
            gate = gate_ref[e, h * HSLOTS:(h + 1) * HSLOTS, e:e + 1]
            sig = jax.nn.sigmoid(a)
            act = a * sig
            hidden = act * b
            dh = gate * back
            d_gate = dh * b * sig * (1.0 + a * (1.0 - sig))
            prob = jnp.sum(hidden * back, axis=1, keepdims=True)
            prob = jnp.where(lane == 0, prob, 0.0)
            d = jnp.concatenate([d_gate, prob, dh * act, side, gate * hidden, side], axis=1).astype(BF16)
            d_ref[e, h * HSLOTS:(h + 1) * HSLOTS, :] = d
            spread = dot(ones(slots == info[:, e:e + 1]), d[:, :PAIR])
            out_ref[:, e * PAIR:(e + 1) * PAIR] = spread.astype(BF16)
            mine = info == (first + e).astype(F32)
            mine = mine & (wide >= IDS_AT) & (wide < IDS_AT + TOP)
            tail = jnp.where(mine, spread[:, FSH:FSH + 1], tail)
        if h == 0:
            tail_ref[...] = tail
    tail = jnp.concatenate([tail, none], axis=1)
    for g in range(NG):
        give_ref[:, g] = dx_of(far_ref[...], wx_ref[g], tail).astype(BF16)


def input_kernel(got_ref, spread_ref, tail_ref, wx_ref, dx_ref):
    none = jnp.zeros((HALF, WIDE - LANES), F32)
    tail = jnp.concatenate([tail_ref[...], none], axis=1)
    for g in range(NG):
        dx = dx_of(spread_ref[...], wx_ref[g], tail) + got_ref[:, g].astype(F32)
        dx_ref[:, g] = dx.astype(BF16)


def weight_kernel(xs_ref, ds_ref, d_ref, out_ref):
    for e in range(NE):
        for g in range(NG):
            both = dot_dims(xs_ref[g, e], d_ref[e, :, :PAIR], 0, 0)
            down = dot_dims(ds_ref[g, e], d_ref[e, :, PAIR:], 0, 0)
            for i, (grad, base) in enumerate(((both, 0), (both, LANES), (down, 0))):
                pieces = [grad[s * STEP:s * STEP + Q, base:base + FSH] for s in range(4)]
                out_ref[g, e, i] = jnp.concatenate(pieces, axis=1).astype(BF16)


def finish_kernel(dx_ref, got_ref, in_ref, probs_ref):
    total = dx_ref[...] + got_ref[...].astype(F32)
    row, column = iota((WIDE, DSH), 0), iota((WIDE, DSH), 1)
    order = ones(feature_of(row) == column)
    in_ref[...] = dot(total.astype(BF16), order).astype(BF16)
    probs_ref[...] = total[:, :LANES].T[IDS_AT:IDS_AT + TOP, :]


def call(kernel, outs, args, scratch=(), scalar=False):
    vmem = pl.BlockSpec(memory_space=pltpu.VMEM)
    specs = [vmem] * len(args)
    if scalar:
        specs[0] = pl.BlockSpec(memory_space=pltpu.SMEM)
    return pl.pallas_call(
        kernel,
        out_shape=[jax.ShapeDtypeStruct(shape, dtype) for shape, dtype in outs],
        in_specs=specs,
        out_specs=[vmem] * len(outs),
        scratch_shapes=[pltpu.VMEM(shape, dtype) for shape, dtype in scratch],
        compiler_params=pltpu.CompilerParams(vmem_limit_bytes=VMEM),
    )(*args)


def exchange(value, axis):
    return lax.all_to_all(value, axis, split_axis=0, concat_axis=0, tiled=True)


def swap(value, axis):
    return lax.ppermute(value, axis, [(0, 1), (1, 0)])


def flip(value, axis, bit):
    return lax.ppermute(value, axis, [(i, i ^ bit) for i in range(lax.axis_size(axis))])


def local(stash, scale_exp, grad_out, route_ids, route_probs, w_gate, w_up, w_down):
    group = lax.axis_index(GROUP).astype(jnp.int32)
    zq = lax.axis_index("zq").astype(jnp.int32)
    me = jnp.stack([group] + [zq ^ s for s in range(4)])
    small = [v.T for v in (scale_exp, route_ids, route_probs)]
    (xin,) = call(prepare_kernel, [((SHARD, COLS), BF16)], (stash, small[0], grad_out, small[1], small[2]))
    with jax.named_scope("gather_tokens"):
        other = swap(xin, "zh")
        a0 = exchange(jnp.tile(xin, (NX * NG, 1)), ("x",) + GROUP).reshape(NX, NG, SHARD, COLS)
        other, a0 = lax.optimization_barrier((other, a0))
        b0 = exchange(jnp.tile(other, (NX * NG, 1)), ("x",) + GROUP).reshape(NX, NG, SHARD, COLS)
        a1 = swap(a0, "core")
        b1 = swap(b0, "core")
    with jax.named_scope("move_weights"):
        tiles = [w.reshape(EXPERTS, 1, Q, 4 * FSH) for w in (w_gate, w_up, w_down)]
        weights, b0 = lax.optimization_barrier((jnp.concatenate(tiles, axis=1), b0))
        weights = exchange(weights, GROUP).reshape(NG, NE, 3, Q, 4 * FSH)
    rows = ((NG, NE, SLOTS, WIDE), BF16)
    xs, ds, gate, slot = call(
        select_kernel,
        [rows, rows, ((NE, SLOTS, LANES), F32), ((TOKENS, LANES), F32)],
        (me, a0, b0, a1, b1),
        [((2, HALF, HALF), BF16)],
        True)
    part = ((PART, PACK), BF16)
    keep, give1, give2, give3, wx = call(
        forward_kernel,
        [((PART, PACK), F32), part, part, part, ((NG, WIDE, NE * PAIR), BF16)],
        (me, weights, xs, ds),
        [((NG, WIDE, NE * LANES), BF16), ((HSLOTS, PACK), F32)],
        True)
    with jax.named_scope("sum_pre"):
        got = [flip(give, "zq", 1 + i) for i, give in enumerate((give1, give2, give3))]
        pre = (keep + sum(v.astype(F32) for v in got)).astype(BF16)
    with jax.named_scope("spread_pre"):
        pre = [pre] + [flip(pre, "zq", s) for s in range(1, 4)]
    dx_shape = (NX, NG, SHARD, COLS)
    d, spread, tail, give = call(
        middle_kernel,
        [((NE, SLOTS, 3 * LANES), BF16), ((HALF, NE * PAIR), BF16), ((HALF, LANES), F32), (dx_shape, BF16)],
        (me, *pre, wx, gate, slot),
        [((HSLOTS, PACK), F32), ((HALF, NE * PAIR), BF16)],
        True)
    with jax.named_scope("sum_dx"):
        (dx,) = call(input_kernel, [(dx_shape, BF16)], (swap(give, "core"), spread, tail, wx))
        dx, d = lax.optimization_barrier((dx, d))
        dx = exchange(dx.reshape(NX * NG, SHARD, COLS), ("x",) + GROUP)
        dx = jnp.sum(dx.astype(F32), axis=0)
        keep, give = dx[:, :WIDE], dx[:, WIDE:].astype(BF16)
    (grads,) = call(weight_kernel, [((NG, NE, 3, Q, 4 * FSH), BF16)], (xs, ds, d))
    give, grads = lax.optimization_barrier((give, grads))
    got = swap(give, "zh")
    with jax.named_scope("return_grads"):
        grads = exchange(grads.reshape(EXPERTS, 3, Q, 4 * FSH), GROUP)
        grads = [grads[:, i].reshape(w_gate.shape) for i in range(3)]
    keep, *grads = lax.optimization_barrier((keep, *grads))
    grad_in, grad_probs = call(finish_kernel, [((SHARD, DSH), BF16), ((TOP, SHARD), F32)], (keep, got))
    return (grad_in, grad_probs.T, *grads)


def solution(mesh):
    fine = Mesh(mesh.devices.reshape(4, 2, 2, 4, 2, 4), DP + EX)
    weight = P(None, DP + EX)
    in_specs = (P(DP, EX), P(DP, EX), P(DP, EX), P(DP, None), P(DP, None), weight, weight, weight)
    out_specs = (P(DP, EX), P(DP, None), weight, weight, weight)
    return jax.shard_map(local, mesh=fine, in_specs=in_specs, out_specs=out_specs, check_vma=False)
```

```python
import jax
import jax.numpy as jnp
from jax import lax
from jax.experimental import pallas as pl
from jax.experimental.pallas import tpu as pltpu
from jax.sharding import Mesh, PartitionSpec as P

DP = ("x", "zh", "core")
EX = ("zq", "zp", "y")
GROUP = ("zp", "y")
BLK = 16
TOP = 6
CAP = 8
EXPERTS = 16
DSH = 160
FSH = 96
SHARD = 32
TOKENS = 512
BLOCKS = TOKENS // BLK
LANES = 128
NG = 8
NE = EXPERTS // NG
NX = 4
SLOTS = BLOCKS * CAP
HALF = TOKENS // 2
HSLOTS = SLOTS // 2
PART = HSLOTS // 4
Q = DSH // 4
STEP = Q + 8
WIDE = 4 * STEP
COLS = 2 * WIDE
IDS_AT = Q
PROBS_AT = STEP + Q
TRIO = 3 * FSH
PACK = 2 * NE * TRIO
PAIR = 2 * LANES
VMEM = 56 * 1024 * 1024
BF16 = jnp.bfloat16
F32 = jnp.float32


def iota(shape, dim):
    return lax.broadcasted_iota(jnp.int32, shape, dim)


def dot(a, b):
    return jnp.dot(a, b, preferred_element_type=F32)


def dot_dims(a, b, left, right):
    return lax.dot_general(a, b, (((left,), (right,)), ((), ())), preferred_element_type=F32)


def feature_of(column):
    s = sum(jnp.where(column >= i * STEP, 1, 0) for i in range(1, 4))
    q = column - s * STEP
    return jnp.where((q < Q) & (column >= 0) & (column < WIDE), 4 * q + s, -1)


def ones(mask):
    return jnp.where(mask, 1.0, 0.0).astype(BF16)


def prepare_kernel(stash_ref, scale_ref, dy_ref, ids_ref, probs_ref, out_ref):
    scale = scale_ref[...]
    factor = jnp.where(scale == -2, 0.25, jnp.where(scale == -1, 0.5, jnp.where(scale == 0, 1.0, 2.0)))
    per = DSH // scale.shape[0]
    shape = (scale.shape[0], DSH)
    first = iota(shape, 0) * per
    expand = ones((iota(shape, 1) >= first) & (iota(shape, 1) < first + per))
    x = (stash_ref[...].astype(F32) * dot_dims(factor.astype(BF16), expand, 0, 0)).astype(BF16)
    row, column = iota((DSH, COLS), 0), iota((DSH, COLS), 1)
    out = dot(x, ones(row == feature_of(column)))
    out = out + dot(dy_ref[...], ones(row == feature_of(column - WIDE)))
    row, column = iota((TOP, COLS), 0), iota((TOP, COLS), 1)
    out = out + dot_dims(ids_ref[...].astype(F32).astype(BF16), ones(row == column - IDS_AT), 0, 0)
    out = out + dot_dims(probs_ref[...], ones(row == column - PROBS_AT), 0, 0)
    out_ref[...] = out.astype(BF16)


def select_kernel(me_ref, x0_ref, x1_ref, xs_ref, ds_ref, gate_ref, slot_ref, pick_ref):
    first = me_ref[0] * NE
    lane = iota((HALF, LANES), 1)
    row, column = iota((HALF, HALF), 0), iota((HALF, HALF), 1)
    before = ones((column < row) & (column >= row - row % BLK))
    block = (iota((HALF, LANES), 0) // BLK).astype(F32)
    row = iota((HSLOTS, HALF), 0).astype(F32)

    def tokens(x_ref, g, lanes):
        return x_ref[:, g, :, lanes].reshape(HALF, lanes.stop - lanes.start)

    for h, x_ref in enumerate((x0_ref, x1_ref)):
        at = slice(h * HALF, (h + 1) * HALF)
        head = tokens(x_ref, 0, slice(0, LANES)).astype(F32)
        hit = jnp.zeros((HALF, LANES), F32)
        prob = jnp.zeros((HALF, LANES), F32)
        for k in range(TOP):
            same = head[:, IDS_AT + k:IDS_AT + k + 1] == (lane + first).astype(F32)
            hit = jnp.where(same, 1.0, hit)
            prob = jnp.where(same, head[:, PROBS_AT + k:PROBS_AT + k + 1], prob)
        place = dot(before, hit.astype(BF16))
        slot = jnp.where(hit > 0.5, block * CAP + place, -1.0)
        slot_ref[at, :] = jnp.where(lane < NE, slot, head)
        slot_t = slot.T
        for e in range(NE):
            pick_ref[h, e * HSLOTS:(e + 1) * HSLOTS, :] = ones(row == slot_t[e:e + 1, :])
        gate = dot(pick_ref[h], prob.astype(BF16))
        for e in range(NE):
            gate_ref[e, h * HSLOTS:(h + 1) * HSLOTS, :] = gate[e * HSLOTS:(e + 1) * HSLOTS]
    for g in range(NG):
        for h, x_ref in enumerate((x0_ref, x1_ref)):
            x = dot(pick_ref[h], tokens(x_ref, g, slice(0, WIDE))).astype(BF16)
            dy = dot(pick_ref[h], tokens(x_ref, g, slice(WIDE, COLS))).astype(BF16)
            at = slice(h * HSLOTS, (h + 1) * HSLOTS)
            for e in range(NE):
                xs_ref[g, e, at, :] = x[e * HSLOTS:(e + 1) * HSLOTS]
                ds_ref[g, e, at, :] = dy[e * HSLOTS:(e + 1) * HSLOTS]


def forward_kernel(me_ref, w_ref, xs_ref, ds_ref, keep_ref, give1_ref, give2_ref, give3_ref, wx_ref, wd_ref, pre_ref):
    low = jnp.zeros((STEP - Q, FSH), F32)
    side = jnp.zeros((STEP, LANES - FSH), F32)
    for g in range(NG):
        for e in range(NE):
            for i in range(3):
                w = w_ref[g, e, i].astype(F32)
                for s in range(4):
                    piece = jnp.concatenate([w[:, s * FSH:(s + 1) * FSH], low], axis=0)
                    piece = jnp.concatenate([piece, side], axis=1).astype(BF16)
                    if i < 2:
                        wx_ref[g, s * STEP:(s + 1) * STEP, e * PAIR + i * LANES:e * PAIR + (i + 1) * LANES] = piece
                    else:
                        wd_ref[g, s * STEP:(s + 1) * STEP, e * LANES:(e + 1) * LANES] = piece
    for e in range(NE):
        ab = jnp.zeros((SLOTS, PAIR), F32)
        back = jnp.zeros((SLOTS, LANES), F32)
        for g in range(NG):
            ab = ab + dot(xs_ref[g, e], wx_ref[g, :, e * PAIR:(e + 1) * PAIR])
            back = back + dot(ds_ref[g, e], wd_ref[g, :, e * LANES:(e + 1) * LANES])
        trio = jnp.concatenate([ab[:, :FSH], ab[:, LANES:LANES + FSH], back[:, :FSH]], axis=1)
        for h in range(2):
            unit = 2 * e + h
            pre_ref[:, unit * TRIO:(unit + 1) * TRIO] = trio[h * HSLOTS:(h + 1) * HSLOTS]
    for s, out_ref in enumerate((keep_ref, give1_ref, give2_ref, give3_ref)):
        rows = pl.ds(pl.multiple_of(me_ref[1 + s] * PART, PART), PART)
        out_ref[...] = pre_ref[rows, :].astype(out_ref.dtype)


def dx_of(spread, wx, tail):
    dx = dot_dims(spread, wx, 1, 1) + tail
    dx = dx.reshape(NX, 2, SHARD, WIDE)
    return jnp.concatenate([dx[:, 0], dx[:, 1]], axis=2)


def middle_kernel(me_ref, own_ref, pre1_ref, pre2_ref, pre3_ref, wx_ref, gate_ref, slot_ref,
                  d_ref, spread_ref, tail_ref, give_ref, pre_ref, far_ref):
    first = me_ref[0] * NE
    for s, part_ref in enumerate((own_ref, pre1_ref, pre2_ref, pre3_ref)):
        rows = pl.ds(pl.multiple_of(me_ref[1 + s] * PART, PART), PART)
        pre_ref[rows, :] = part_ref[...].astype(F32)
    side = jnp.zeros((HSLOTS, LANES - FSH), F32)
    lane = iota((HSLOTS, LANES - FSH), 1)
    slots = iota((HALF, HSLOTS), 1).astype(F32)
    wide = iota((HALF, LANES), 1)
    none = jnp.zeros((HALF, WIDE - LANES), F32)
    for h, out_ref in enumerate((spread_ref, far_ref)):
        info = slot_ref[h * HALF:(h + 1) * HALF, :]
        tail = jnp.zeros((HALF, LANES), F32)
        for e in range(NE):
            base = (2 * e + h) * TRIO
            pre = pre_ref[:, base:base + TRIO]
            a, b, back = (pre[:, i * FSH:(i + 1) * FSH] for i in range(3))
            gate = gate_ref[e, h * HSLOTS:(h + 1) * HSLOTS, e:e + 1]
            sig = jax.nn.sigmoid(a)
            act = a * sig
            hidden = act * b
            dh = gate * back
            d_gate = dh * b * sig * (1.0 + a * (1.0 - sig))
            prob = jnp.sum(hidden * back, axis=1, keepdims=True)
            prob = jnp.where(lane == 0, prob, 0.0)
            d = jnp.concatenate([d_gate, prob, dh * act, side, gate * hidden, side], axis=1).astype(BF16)
            d_ref[e, h * HSLOTS:(h + 1) * HSLOTS, :] = d
            spread = dot(ones(slots == info[:, e:e + 1]), d[:, :PAIR])
            out_ref[:, e * PAIR:(e + 1) * PAIR] = spread.astype(BF16)
            mine = info == (first + e).astype(F32)
            mine = mine & (wide >= IDS_AT) & (wide < IDS_AT + TOP)
            tail = jnp.where(mine, spread[:, FSH:FSH + 1], tail)
        if h == 0:
            tail_ref[...] = tail
    tail = jnp.concatenate([tail, none], axis=1)
    for g in range(NG):
        give_ref[:, g] = dx_of(far_ref[...], wx_ref[g], tail).astype(BF16)


def input_kernel(got_ref, spread_ref, tail_ref, wx_ref, dx_ref):
    none = jnp.zeros((HALF, WIDE - LANES), F32)
    tail = jnp.concatenate([tail_ref[...], none], axis=1)
    for g in range(NG):
        dx = dx_of(spread_ref[...], wx_ref[g], tail) + got_ref[:, g].astype(F32)
        dx_ref[:, g] = dx.astype(BF16)


def weight_kernel(xs_ref, ds_ref, d_ref, out_ref):
    for e in range(NE):
        for g in range(NG):
            both = dot_dims(xs_ref[g, e], d_ref[e, :, :PAIR], 0, 0)
            down = dot_dims(ds_ref[g, e], d_ref[e, :, PAIR:], 0, 0)
            for i, (grad, base) in enumerate(((both, 0), (both, LANES), (down, 0))):
                pieces = [grad[s * STEP:s * STEP + Q, base:base + FSH] for s in range(4)]
                out_ref[g, e, i] = jnp.concatenate(pieces, axis=1).astype(BF16)


def finish_kernel(dx_ref, got_ref, in_ref, probs_ref):
    total = dx_ref[...] + got_ref[...].astype(F32)
    row, column = iota((WIDE, DSH), 0), iota((WIDE, DSH), 1)
    order = ones(feature_of(row) == column)
    in_ref[...] = dot(total.astype(BF16), order).astype(BF16)
    probs_ref[...] = total[:, :LANES].T[IDS_AT:IDS_AT + TOP, :]


def call(kernel, outs, args, scratch=(), scalar=False):
    vmem = pl.BlockSpec(memory_space=pltpu.VMEM)
    specs = [vmem] * len(args)
    if scalar:
        specs[0] = pl.BlockSpec(memory_space=pltpu.SMEM)
    return pl.pallas_call(
        kernel,
        out_shape=[jax.ShapeDtypeStruct(shape, dtype) for shape, dtype in outs],
        in_specs=specs,
        out_specs=[vmem] * len(outs),
        scratch_shapes=[pltpu.VMEM(shape, dtype) for shape, dtype in scratch],
        compiler_params=pltpu.CompilerParams(vmem_limit_bytes=VMEM),
    )(*args)


def exchange(value, axis):
    return lax.all_to_all(value, axis, split_axis=0, concat_axis=0, tiled=True)


def swap(value, axis):
    return lax.ppermute(value, axis, [(0, 1), (1, 0)])


def flip(value, axis, bit):
    return lax.ppermute(value, axis, [(i, i ^ bit) for i in range(lax.axis_size(axis))])


def local(stash, scale_exp, grad_out, route_ids, route_probs, w_gate, w_up, w_down):
    group = lax.axis_index(GROUP).astype(jnp.int32)
    zq = lax.axis_index("zq").astype(jnp.int32)
    me = jnp.stack([group] + [zq ^ s for s in range(4)])
    small = [v.T for v in (scale_exp, route_ids, route_probs)]
    (xin,) = call(prepare_kernel, [((SHARD, COLS), BF16)], (stash, small[0], grad_out, small[1], small[2]))
    with jax.named_scope("gather_tokens"):
        xin = jnp.concatenate([xin, swap(xin, "zh")])
        x0 = exchange(jnp.tile(xin, (NX * NG, 1)), ("x",) + GROUP).reshape(NX, NG, 2 * SHARD, COLS)
        x1 = swap(x0, "core")
    with jax.named_scope("move_weights"):
        tiles = [w.reshape(EXPERTS, 1, Q, 4 * FSH) for w in (w_gate, w_up, w_down)]
        weights, x0 = lax.optimization_barrier((jnp.concatenate(tiles, axis=1), x0))
        weights = exchange(weights, GROUP).reshape(NG, NE, 3, Q, 4 * FSH)
    rows = ((NG, NE, SLOTS, WIDE), BF16)
    xs, ds, gate, slot = call(
        select_kernel,
        [rows, rows, ((NE, SLOTS, LANES), F32), ((TOKENS, LANES), F32)],
        (me, x0, x1),
        [((2, HALF, HALF), BF16)],
        True)
    part = ((PART, PACK), BF16)
    keep, give1, give2, give3, wx = call(
        forward_kernel,
        [((PART, PACK), F32), part, part, part, ((NG, WIDE, NE * PAIR), BF16)],
        (me, weights, xs, ds),
        [((NG, WIDE, NE * LANES), BF16), ((HSLOTS, PACK), F32)],
        True)
    with jax.named_scope("sum_pre"):
        got = [flip(give, "zq", 1 + i) for i, give in enumerate((give1, give2, give3))]
        pre = (keep + sum(v.astype(F32) for v in got)).astype(BF16)
    with jax.named_scope("spread_pre"):
        pre = [pre] + [flip(pre, "zq", s) for s in range(1, 4)]
    dx_shape = (NX, NG, SHARD, COLS)
    d, spread, tail, give = call(
        middle_kernel,
        [((NE, SLOTS, 3 * LANES), BF16), ((HALF, NE * PAIR), BF16), ((HALF, LANES), F32), (dx_shape, BF16)],
        (me, *pre, wx, gate, slot),
        [((HSLOTS, PACK), F32), ((HALF, NE * PAIR), BF16)],
        True)
    with jax.named_scope("sum_dx"):
        (dx,) = call(input_kernel, [(dx_shape, BF16)], (swap(give, "core"), spread, tail, wx))
        dx, d = lax.optimization_barrier((dx, d))
        dx = exchange(dx.reshape(NX * NG, SHARD, COLS), ("x",) + GROUP)
        dx = jnp.sum(dx.astype(F32), axis=0)
        keep, give = dx[:, :WIDE], dx[:, WIDE:].astype(BF16)
    (grads,) = call(weight_kernel, [((NG, NE, 3, Q, 4 * FSH), BF16)], (xs, ds, d))
    give, grads = lax.optimization_barrier((give, grads))
    got = swap(give, "zh")
    with jax.named_scope("return_grads"):
        grads = exchange(grads.reshape(EXPERTS, 3, Q, 4 * FSH), GROUP)
        grads = [grads[:, i].reshape(w_gate.shape) for i in range(3)]
    keep, *grads = lax.optimization_barrier((keep, *grads))
    grad_in, grad_probs = call(finish_kernel, [((SHARD, DSH), BF16), ((TOP, SHARD), F32)], (keep, got))
    return (grad_in, grad_probs.T, *grads)


def solution(mesh):
    fine = Mesh(mesh.devices.reshape(4, 2, 2, 4, 2, 4), DP + EX)
    weight = P(None, DP + EX)
    in_specs = (P(DP, EX), P(DP, EX), P(DP, EX), P(DP, None), P(DP, None), weight, weight, weight)
    out_specs = (P(DP, EX), P(DP, None), weight, weight, weight)
    return jax.shard_map(local, mesh=fine, in_specs=in_specs, out_specs=out_specs, check_vma=False)
```

```python
import jax
import jax.numpy as jnp
from jax import lax
from jax.experimental import pallas as pl
from jax.experimental.pallas import tpu as pltpu
from jax.sharding import Mesh, PartitionSpec as P

DP = ("x", "zh", "core")
EX = ("zq", "zp", "y")
GROUP = ("zp", "y")
BLK = 16
TOP = 6
CAP = 8
EXPERTS = 16
DSH = 160
FSH = 96
SHARD = 32
TOKENS = 512
BLOCKS = TOKENS // BLK
LANES = 128
NG = 8
NE = EXPERTS // NG
NX = 4
SLOTS = BLOCKS * CAP
HALF = TOKENS // 2
HSLOTS = SLOTS // 2
PART = HSLOTS // 4
Q = DSH // 4
STEP = Q + 8
WIDE = 4 * STEP
COLS = 2 * WIDE
IDS_AT = Q
PROBS_AT = STEP + Q
TRIO = 3 * FSH
PACK = 2 * NE * TRIO
PAIR = 2 * LANES
VMEM = 24 * 1024 * 1024
BF16 = jnp.bfloat16
F32 = jnp.float32


def iota(shape, dim):
    return lax.broadcasted_iota(jnp.int32, shape, dim)


def dot(a, b):
    return jnp.dot(a, b, preferred_element_type=F32)


def dot_dims(a, b, left, right):
    return lax.dot_general(a, b, (((left,), (right,)), ((), ())), preferred_element_type=F32)


def fetch(sources, targets, sems):
    copies = [pltpu.make_async_copy(a, b, sems.at[i]) for i, (a, b) in enumerate(zip(sources, targets))]
    for copy in copies:
        copy.start()
    return copies


def feature_of(column):
    s = sum(jnp.where(column >= i * STEP, 1, 0) for i in range(1, 4))
    q = column - s * STEP
    return jnp.where((q < Q) & (column >= 0) & (column < WIDE), 4 * q + s, -1)


def ones(mask):
    return jnp.where(mask, 1.0, 0.0).astype(BF16)


def prepare_kernel(stash_ref, scale_ref, dy_ref, ids_ref, probs_ref, out_ref):
    scale = scale_ref[...]
    factor = jnp.where(scale == -2, 0.25, jnp.where(scale == -1, 0.5, jnp.where(scale == 0, 1.0, 2.0)))
    per = DSH // scale.shape[0]
    shape = (scale.shape[0], DSH)
    first = iota(shape, 0) * per
    expand = ones((iota(shape, 1) >= first) & (iota(shape, 1) < first + per))
    x = (stash_ref[...].astype(F32) * dot_dims(factor.astype(BF16), expand, 0, 0)).astype(BF16)
    row, column = iota((DSH, COLS), 0), iota((DSH, COLS), 1)
    out = dot(x, ones(row == feature_of(column)))
    out = out + dot(dy_ref[...], ones(row == feature_of(column - WIDE)))
    row, column = iota((TOP, COLS), 0), iota((TOP, COLS), 1)
    out = out + dot_dims(ids_ref[...].astype(F32).astype(BF16), ones(row == column - IDS_AT), 0, 0)
    out = out + dot_dims(probs_ref[...], ones(row == column - PROBS_AT), 0, 0)
    out_ref[...] = out.astype(BF16)


def select_kernel(me_ref, x0_ref, x1_ref, xs_ref, ds_ref, gate_ref, slot_ref, pick_ref):
    first = me_ref[0] * NE
    lane = iota((HALF, LANES), 1)
    row, column = iota((HALF, HALF), 0), iota((HALF, HALF), 1)
    before = ones((column < row) & (column >= row - row % BLK))
    block = (iota((HALF, LANES), 0) // BLK).astype(F32)
    row = iota((HSLOTS, HALF), 0).astype(F32)

    def tokens(x_ref, g, lanes):
        return x_ref[:, g, :, lanes].reshape(HALF, lanes.stop - lanes.start)

    for h, x_ref in enumerate((x0_ref, x1_ref)):
        at = slice(h * HALF, (h + 1) * HALF)
        head = tokens(x_ref, 0, slice(0, LANES)).astype(F32)
        hit = jnp.zeros((HALF, LANES), F32)
        prob = jnp.zeros((HALF, LANES), F32)
        for k in range(TOP):
            same = head[:, IDS_AT + k:IDS_AT + k + 1] == (lane + first).astype(F32)
            hit = jnp.where(same, 1.0, hit)
            prob = jnp.where(same, head[:, PROBS_AT + k:PROBS_AT + k + 1], prob)
        place = dot(before, hit.astype(BF16))
        slot = jnp.where(hit > 0.5, block * CAP + place, -1.0)
        slot_ref[at, :] = jnp.where(lane < NE, slot, head)
        slot_t = slot.T
        for e in range(NE):
            pick_ref[h, e * HSLOTS:(e + 1) * HSLOTS, :] = ones(row == slot_t[e:e + 1, :])
        gate = dot(pick_ref[h], prob.astype(BF16))
        for e in range(NE):
            gate_ref[e, h * HSLOTS:(h + 1) * HSLOTS, :] = gate[e * HSLOTS:(e + 1) * HSLOTS]
    for g in range(NG):
        for h, x_ref in enumerate((x0_ref, x1_ref)):
            x = dot(pick_ref[h], tokens(x_ref, g, slice(0, WIDE))).astype(BF16)
            dy = dot(pick_ref[h], tokens(x_ref, g, slice(WIDE, COLS))).astype(BF16)
            at = slice(h * HSLOTS, (h + 1) * HSLOTS)
            for e in range(NE):
                xs_ref[g, e, at, :] = x[e * HSLOTS:(e + 1) * HSLOTS]
                ds_ref[g, e, at, :] = dy[e * HSLOTS:(e + 1) * HSLOTS]


def forward_kernel(me_ref, *refs):
    (keep_ref, give1_ref, give2_ref, give3_ref, wx_ref, wd_ref, pre_ref, w_ref, xs_ref, ds_ref, sems) = refs[3:]
    copies = fetch(refs[:3], (w_ref, xs_ref, ds_ref), sems)
    copies[0].wait()
    low = jnp.zeros((STEP - Q, FSH), F32)
    side = jnp.zeros((STEP, LANES - FSH), F32)
    for g in range(NG):
        every = w_ref[g].astype(F32)
        for e in range(NE):
            for i in range(3):
                w = every[(3 * e + i) * Q:(3 * e + i + 1) * Q]
                for s in range(4):
                    piece = jnp.concatenate([w[:, s * FSH:(s + 1) * FSH], low], axis=0)
                    piece = jnp.concatenate([piece, side], axis=1).astype(BF16)
                    if i < 2:
                        wx_ref[g, s * STEP:(s + 1) * STEP, e * PAIR + i * LANES:e * PAIR + (i + 1) * LANES] = piece
                    else:
                        wd_ref[g, s * STEP:(s + 1) * STEP, e * LANES:(e + 1) * LANES] = piece
    copies[1].wait()
    copies[2].wait()
    for e in range(NE):
        ab = jnp.zeros((SLOTS, PAIR), F32)
        back = jnp.zeros((SLOTS, LANES), F32)
        for g in range(NG):
            ab = ab + dot(xs_ref[g, e], wx_ref[g, :, e * PAIR:(e + 1) * PAIR])
            back = back + dot(ds_ref[g, e], wd_ref[g, :, e * LANES:(e + 1) * LANES])
        trio = jnp.concatenate([ab[:, :FSH], ab[:, LANES:LANES + FSH], back[:, :FSH]], axis=1)
        for h in range(2):
            unit = 2 * e + h
            pre_ref[:, unit * TRIO:(unit + 1) * TRIO] = trio[h * HSLOTS:(h + 1) * HSLOTS]
    for s, out_ref in enumerate((keep_ref, give1_ref, give2_ref, give3_ref)):
        rows = pl.ds(pl.multiple_of(me_ref[1 + s] * PART, PART), PART)
        out_ref[...] = pre_ref[rows, :].astype(out_ref.dtype)


def dx_of(spread, wx, tail):
    dx = dot_dims(spread, wx, 1, 1) + tail
    dx = dx.reshape(NX, 2, SHARD, WIDE)
    return jnp.concatenate([dx[:, 0], dx[:, 1]], axis=2)


def middle_kernel(me_ref, *refs):
    (d_ref, spread_ref, tail_ref, give_ref, pre_ref, far_ref, *local_refs, sems) = refs[7:]
    (gate_ref, slot_ref, wx_ref), parts = local_refs[4:], local_refs[:4]
    copies = fetch(refs[:7], local_refs, sems)
    first = me_ref[0] * NE
    for s, part_ref in enumerate(parts):
        rows = pl.ds(pl.multiple_of(me_ref[1 + s] * PART, PART), PART)
        copies[s].wait()
        pre_ref[rows, :] = part_ref[...].astype(F32)
    copies[4].wait()
    copies[5].wait()
    side = jnp.zeros((HSLOTS, LANES - FSH), F32)
    lane = iota((HSLOTS, LANES - FSH), 1)
    slots = iota((HALF, HSLOTS), 1).astype(F32)
    wide = iota((HALF, LANES), 1)
    none = jnp.zeros((HALF, WIDE - LANES), F32)
    for h, out_ref in enumerate((spread_ref, far_ref)):
        info = slot_ref[h * HALF:(h + 1) * HALF, :]
        tail = jnp.zeros((HALF, LANES), F32)
        for e in range(NE):
            base = (2 * e + h) * TRIO
            pre = pre_ref[:, base:base + TRIO]
            a, b, back = (pre[:, i * FSH:(i + 1) * FSH] for i in range(3))
            gate = gate_ref[e, h * HSLOTS:(h + 1) * HSLOTS, e:e + 1]
            sig = jax.nn.sigmoid(a)
            act = a * sig
            hidden = act * b
            dh = gate * back
            d_gate = dh * b * sig * (1.0 + a * (1.0 - sig))
            prob = jnp.sum(hidden * back, axis=1, keepdims=True)
            prob = jnp.where(lane == 0, prob, 0.0)
            d = jnp.concatenate([d_gate, prob, dh * act, side, gate * hidden, side], axis=1).astype(BF16)
            d_ref[e, h * HSLOTS:(h + 1) * HSLOTS, :] = d
            spread = dot(ones(slots == info[:, e:e + 1]), d[:, :PAIR])
            out_ref[:, e * PAIR:(e + 1) * PAIR] = spread.astype(BF16)
            mine = info == (first + e).astype(F32)
            mine = mine & (wide >= IDS_AT) & (wide < IDS_AT + TOP)
            tail = jnp.where(mine, spread[:, FSH:FSH + 1], tail)
        if h == 0:
            tail_ref[...] = tail
    tail = jnp.concatenate([tail, none], axis=1)
    copies[6].wait()
    for g in range(NG):
        give_ref[:, g] = dx_of(far_ref[...], wx_ref[g], tail).astype(BF16)


def input_kernel(*refs):
    dx_ref, spread_ref, tail_ref, wx_ref, got_ref, sems = refs[4:]
    for copy in fetch(refs[:4], (spread_ref, tail_ref, wx_ref, got_ref), sems):
        copy.wait()
    none = jnp.zeros((HALF, WIDE - LANES), F32)
    tail = jnp.concatenate([tail_ref[...], none], axis=1)
    for g in range(NG):
        dx = dx_of(spread_ref[...], wx_ref[g], tail) + got_ref[:, g].astype(F32)
        dx_ref[:, g] = dx.astype(BF16)


def weight_kernel(xs_ref, ds_ref, d_ref, out_ref):
    for e in range(NE):
        for g in range(NG):
            both = dot_dims(xs_ref[g, e], d_ref[e, :, :PAIR], 0, 0)
            down = dot_dims(ds_ref[g, e], d_ref[e, :, PAIR:], 0, 0)
            for i, (grad, base) in enumerate(((both, 0), (both, LANES), (down, 0))):
                pieces = [grad[s * STEP:s * STEP + Q, base:base + FSH] for s in range(4)]
                out_ref[g, e, i] = jnp.concatenate(pieces, axis=1).astype(BF16)


def finish_kernel(dx_any, got_any, in_ref, probs_ref, dx_ref, got_ref, sems):
    for copy in fetch((dx_any, got_any), (dx_ref, got_ref), sems):
        copy.wait()
    total = dx_ref[...] + got_ref[...].astype(F32)
    row, column = iota((WIDE, DSH), 0), iota((WIDE, DSH), 1)
    order = ones(feature_of(row) == column)
    in_ref[...] = dot(total.astype(BF16), order).astype(BF16)
    probs_ref[...] = total[:, :LANES].T[IDS_AT:IDS_AT + TOP, :]


def call(kernel, outs, args, scratch=(), scalar=False, by_hand=False):
    vmem = pl.BlockSpec(memory_space=pltpu.VMEM)
    specs = [pl.BlockSpec(memory_space=pl.ANY) if by_hand else vmem] * len(args)
    if scalar:
        specs[0] = pl.BlockSpec(memory_space=pltpu.SMEM)
    scratch_shapes = [pltpu.VMEM(shape, dtype) for shape, dtype in scratch]
    if by_hand:
        fetched = args[1:] if scalar else args
        scratch_shapes += [pltpu.VMEM(v.shape, v.dtype) for v in fetched]
        scratch_shapes.append(pltpu.SemaphoreType.DMA((len(fetched),)))
    return pl.pallas_call(
        kernel,
        out_shape=[jax.ShapeDtypeStruct(shape, dtype) for shape, dtype in outs],
        in_specs=specs,
        out_specs=[vmem] * len(outs),
        scratch_shapes=scratch_shapes,
        compiler_params=pltpu.CompilerParams(vmem_limit_bytes=VMEM),
    )(*args)


def exchange(value, axis):
    return lax.all_to_all(value, axis, split_axis=0, concat_axis=0, tiled=True)


def swap(value, axis):
    return lax.ppermute(value, axis, [(0, 1), (1, 0)])


def flip(value, axis, bit):
    return lax.ppermute(value, axis, [(i, i ^ bit) for i in range(lax.axis_size(axis))])


def local(stash, scale_exp, grad_out, route_ids, route_probs, w_gate, w_up, w_down):
    group = lax.axis_index(GROUP).astype(jnp.int32)
    zq = lax.axis_index("zq").astype(jnp.int32)
    me = jnp.stack([group] + [zq ^ s for s in range(4)])
    small = [v.T for v in (scale_exp, route_ids, route_probs)]
    (xin,) = call(prepare_kernel, [((SHARD, COLS), BF16)], (stash, small[0], grad_out, small[1], small[2]))
    with jax.named_scope("gather_tokens"):
        xin = jnp.concatenate([xin, swap(xin, "zh")])
        x0 = exchange(jnp.tile(xin, (NX * NG, 1)), ("x",) + GROUP).reshape(NX, NG, 2 * SHARD, COLS)
        x1 = swap(x0, "core")
    with jax.named_scope("move_weights"):
        tiles = [w.reshape(EXPERTS, 1, Q, 4 * FSH) for w in (w_gate, w_up, w_down)]
        weights, x0 = lax.optimization_barrier((jnp.concatenate(tiles, axis=1), x0))
        weights = exchange(weights, GROUP).reshape(NG, NE * 3 * Q, 4 * FSH)
    rows = ((NG, NE, SLOTS, WIDE), BF16)
    xs, ds, gate, slot = call(
        select_kernel,
        [rows, rows, ((NE, SLOTS, LANES), F32), ((TOKENS, LANES), F32)],
        (me, x0, x1),
        [((2, HALF, HALF), BF16)],
        True)
    part = ((PART, PACK), BF16)
    keep, give1, give2, give3, wx = call(
        forward_kernel,
        [((PART, PACK), F32), part, part, part, ((NG, WIDE, NE * PAIR), BF16)],
        (me, weights, xs, ds),
        [((NG, WIDE, NE * LANES), BF16), ((HSLOTS, PACK), F32)],
        True, True)
    with jax.named_scope("sum_pre"):
        got = [flip(give, "zq", 1 + i) for i, give in enumerate((give1, give2, give3))]
        pre = (keep + sum(v.astype(F32) for v in got)).astype(BF16)
    with jax.named_scope("spread_pre"):
        pre = [pre] + [flip(pre, "zq", s) for s in range(1, 4)]
    dx_shape = (NX, NG, SHARD, COLS)
    d, spread, tail, give = call(
        middle_kernel,
        [((NE, SLOTS, 3 * LANES), BF16), ((HALF, NE * PAIR), BF16), ((HALF, LANES), F32), (dx_shape, BF16)],
        (me, *pre, gate, slot, wx),
        [((HSLOTS, PACK), F32), ((HALF, NE * PAIR), BF16)],
        True, True)
    with jax.named_scope("sum_dx"):
        (dx,) = call(input_kernel, [(dx_shape, BF16)], (spread, tail, wx, swap(give, "core")), by_hand=True)
        dx, d = lax.optimization_barrier((dx, d))
        dx = exchange(dx.reshape(NX * NG, SHARD, COLS), ("x",) + GROUP)
        dx = jnp.sum(dx.astype(F32), axis=0)
        keep, give = dx[:, :WIDE], dx[:, WIDE:].astype(BF16)
    (grads,) = call(weight_kernel, [((NG, NE, 3, Q, 4 * FSH), BF16)], (xs, ds, d))
    give, grads = lax.optimization_barrier((give, grads))
    got = swap(give, "zh")
    with jax.named_scope("return_grads"):
        grads = exchange(grads.reshape(EXPERTS, 3, Q, 4 * FSH), GROUP)
        grads = [grads[:, i].reshape(w_gate.shape) for i in range(3)]
    keep, *grads = lax.optimization_barrier((keep, *grads))
    grad_in, grad_probs = call(finish_kernel, [((SHARD, DSH), BF16), ((TOP, SHARD), F32)], (keep, got), by_hand=True)
    return (grad_in, grad_probs.T, *grads)


def solution(mesh):
    fine = Mesh(mesh.devices.reshape(4, 2, 2, 4, 2, 4), DP + EX)
    weight = P(None, DP + EX)
    in_specs = (P(DP, EX), P(DP, EX), P(DP, EX), P(DP, None), P(DP, None), weight, weight, weight)
    out_specs = (P(DP, EX), P(DP, None), weight, weight, weight)
    return jax.shard_map(local, mesh=fine, in_specs=in_specs, out_specs=out_specs, check_vma=False)
```

```python
import jax
import jax.numpy as jnp
from jax import lax
from jax.experimental import pallas as pl
from jax.experimental.pallas import tpu as pltpu
from jax.sharding import Mesh, PartitionSpec as P

DP = ("x", "zh", "core")
EX = ("zq", "zp", "y")
GROUP = ("zp", "y")
BLK = 16
TOP = 6
CAP = 8
EXPERTS = 16
DSH = 160
FSH = 96
SHARD = 32
TOKENS = 512
BLOCKS = TOKENS // BLK
LANES = 128
NG = 8
NE = EXPERTS // NG
NX = 4
SLOTS = BLOCKS * CAP
HALF = TOKENS // 2
HSLOTS = SLOTS // 2
PART = HSLOTS // 4
Q = DSH // 4
STEP = Q + 8
WIDE = 4 * STEP
COLS = 2 * WIDE
IDS_AT = Q
PROBS_AT = STEP + Q
TRIO = 3 * FSH
PACK = 2 * NE * TRIO
PAIR = 2 * LANES
VMEM = 24 * 1024 * 1024
MOST = 56 * 1024 * 1024
BF16 = jnp.bfloat16
F32 = jnp.float32


def iota(shape, dim):
    return lax.broadcasted_iota(jnp.int32, shape, dim)


def dot(a, b):
    return jnp.dot(a, b, preferred_element_type=F32)


def dot_dims(a, b, left, right):
    return lax.dot_general(a, b, (((left,), (right,)), ((), ())), preferred_element_type=F32)


def fetch(sources, targets, sems):
    copies = [pltpu.make_async_copy(a, b, sems.at[i]) for i, (a, b) in enumerate(zip(sources, targets))]
    for copy in copies:
        copy.start()
    return copies


def feature_of(column):
    s = sum(jnp.where(column >= i * STEP, 1, 0) for i in range(1, 4))
    q = column - s * STEP
    return jnp.where((q < Q) & (column >= 0) & (column < WIDE), 4 * q + s, -1)


def ones(mask):
    return jnp.where(mask, 1.0, 0.0).astype(BF16)


def prepare_kernel(stash_ref, scale_ref, dy_ref, ids_ref, probs_ref, out_ref):
    scale = scale_ref[...]
    factor = jnp.where(scale == -2, 0.25, jnp.where(scale == -1, 0.5, jnp.where(scale == 0, 1.0, 2.0)))
    per = DSH // scale.shape[0]
    shape = (scale.shape[0], DSH)
    first = iota(shape, 0) * per
    expand = ones((iota(shape, 1) >= first) & (iota(shape, 1) < first + per))
    x = (stash_ref[...].astype(F32) * dot_dims(factor.astype(BF16), expand, 0, 0)).astype(BF16)
    row, column = iota((DSH, COLS), 0), iota((DSH, COLS), 1)
    out = dot(x, ones(row == feature_of(column)))
    out = out + dot(dy_ref[...], ones(row == feature_of(column - WIDE)))
    row, column = iota((TOP, COLS), 0), iota((TOP, COLS), 1)
    out = out + dot_dims(ids_ref[...].astype(F32).astype(BF16), ones(row == column - IDS_AT), 0, 0)
    out = out + dot_dims(probs_ref[...], ones(row == column - PROBS_AT), 0, 0)
    out_ref[...] = out.astype(BF16)


def select_kernel(me_ref, x0_ref, x1_ref, xs_ref, ds_ref, gate_ref, slot_ref, pick_ref):
    first = me_ref[0] * NE
    lane = iota((HALF, LANES), 1)
    row, column = iota((HALF, HALF), 0), iota((HALF, HALF), 1)
    before = ones((column < row) & (column >= row - row % BLK))
    block = (iota((HALF, LANES), 0) // BLK).astype(F32)
    row = iota((HSLOTS, HALF), 0).astype(F32)

    def tokens(x_ref, g, lanes):
        return x_ref[:, g, :, lanes].reshape(HALF, lanes.stop - lanes.start)

    for h, x_ref in enumerate((x0_ref, x1_ref)):
        at = slice(h * HALF, (h + 1) * HALF)
        head = tokens(x_ref, 0, slice(0, LANES)).astype(F32)
        hit = jnp.zeros((HALF, LANES), F32)
        prob = jnp.zeros((HALF, LANES), F32)
        for k in range(TOP):
            same = head[:, IDS_AT + k:IDS_AT + k + 1] == (lane + first).astype(F32)
            hit = jnp.where(same, 1.0, hit)
            prob = jnp.where(same, head[:, PROBS_AT + k:PROBS_AT + k + 1], prob)
        place = dot(before, hit.astype(BF16))
        slot = jnp.where(hit > 0.5, block * CAP + place, -1.0)
        slot_ref[at, :] = jnp.where(lane < NE, slot, head)
        slot_t = slot.T
        for e in range(NE):
            pick_ref[h, e * HSLOTS:(e + 1) * HSLOTS, :] = ones(row == slot_t[e:e + 1, :])
        gate = dot(pick_ref[h], prob.astype(BF16))
        for e in range(NE):
            gate_ref[e, h * HSLOTS:(h + 1) * HSLOTS, :] = gate[e * HSLOTS:(e + 1) * HSLOTS]
    for g in range(NG):
        for h, x_ref in enumerate((x0_ref, x1_ref)):
            x = dot(pick_ref[h], tokens(x_ref, g, slice(0, WIDE))).astype(BF16)
            dy = dot(pick_ref[h], tokens(x_ref, g, slice(WIDE, COLS))).astype(BF16)
            at = slice(h * HSLOTS, (h + 1) * HSLOTS)
            for e in range(NE):
                xs_ref[g, e, at, :] = x[e * HSLOTS:(e + 1) * HSLOTS]
                ds_ref[g, e, at, :] = dy[e * HSLOTS:(e + 1) * HSLOTS]


def forward_kernel(me_ref, *refs):
    (keep_ref, give1_ref, give2_ref, give3_ref, wx_ref, wd_ref, pre_ref, w_ref, xs_ref, ds_ref, sems) = refs[3:]
    copies = fetch(refs[:3], (w_ref, xs_ref, ds_ref), sems)
    copies[0].wait()
    low = jnp.zeros((STEP - Q, FSH), F32)
    side = jnp.zeros((STEP, LANES - FSH), F32)
    for g in range(NG):
        every = w_ref[g].astype(F32)
        for e in range(NE):
            for i in range(3):
                w = every[(3 * e + i) * Q:(3 * e + i + 1) * Q]
                for s in range(4):
                    piece = jnp.concatenate([w[:, s * FSH:(s + 1) * FSH], low], axis=0)
                    piece = jnp.concatenate([piece, side], axis=1).astype(BF16)
                    if i < 2:
                        wx_ref[g, s * STEP:(s + 1) * STEP, e * PAIR + i * LANES:e * PAIR + (i + 1) * LANES] = piece
                    else:
                        wd_ref[g, s * STEP:(s + 1) * STEP, e * LANES:(e + 1) * LANES] = piece
    copies[1].wait()
    copies[2].wait()
    for e in range(NE):
        ab = jnp.zeros((SLOTS, PAIR), F32)
        back = jnp.zeros((SLOTS, LANES), F32)
        for g in range(NG):
            ab = ab + dot(xs_ref[g, e], wx_ref[g, :, e * PAIR:(e + 1) * PAIR])
            back = back + dot(ds_ref[g, e], wd_ref[g, :, e * LANES:(e + 1) * LANES])
        trio = jnp.concatenate([ab[:, :FSH], ab[:, LANES:LANES + FSH], back[:, :FSH]], axis=1)
        for h in range(2):
            unit = 2 * e + h
            pre_ref[:, unit * TRIO:(unit + 1) * TRIO] = trio[h * HSLOTS:(h + 1) * HSLOTS]
    for s, out_ref in enumerate((keep_ref, give1_ref, give2_ref, give3_ref)):
        rows = pl.ds(pl.multiple_of(me_ref[1 + s] * PART, PART), PART)
        out_ref[...] = pre_ref[rows, :].astype(out_ref.dtype)


def dx_of(spread, wx, tail):
    dx = dot_dims(spread, wx, 1, 1) + tail
    dx = dx.reshape(NX, 2, SHARD, WIDE)
    return jnp.concatenate([dx[:, 0], dx[:, 1]], axis=2)


def middle_kernel(me_ref, *refs):
    (d_ref, spread_ref, tail_ref, give_ref, pre_ref, far_ref, *local_refs, sems) = refs[7:]
    (gate_ref, slot_ref, wx_ref), parts = local_refs[4:], local_refs[:4]
    copies = fetch(refs[:7], local_refs, sems)
    first = me_ref[0] * NE
    for s, part_ref in enumerate(parts):
        rows = pl.ds(pl.multiple_of(me_ref[1 + s] * PART, PART), PART)
        copies[s].wait()
        pre_ref[rows, :] = part_ref[...].astype(F32)
    copies[4].wait()
    copies[5].wait()
    side = jnp.zeros((HSLOTS, LANES - FSH), F32)
    lane = iota((HSLOTS, LANES - FSH), 1)
    slots = iota((HALF, HSLOTS), 1).astype(F32)
    wide = iota((HALF, LANES), 1)
    none = jnp.zeros((HALF, WIDE - LANES), F32)
    for h, out_ref in enumerate((spread_ref, far_ref)):
        info = slot_ref[h * HALF:(h + 1) * HALF, :]
        tail = jnp.zeros((HALF, LANES), F32)
        for e in range(NE):
            base = (2 * e + h) * TRIO
            pre = pre_ref[:, base:base + TRIO]
            a, b, back = (pre[:, i * FSH:(i + 1) * FSH] for i in range(3))
            gate = gate_ref[e, h * HSLOTS:(h + 1) * HSLOTS, e:e + 1]
            sig = jax.nn.sigmoid(a)
            act = a * sig
            hidden = act * b
            dh = gate * back
            d_gate = dh * b * sig * (1.0 + a * (1.0 - sig))
            prob = jnp.sum(hidden * back, axis=1, keepdims=True)
            prob = jnp.where(lane == 0, prob, 0.0)
            d = jnp.concatenate([d_gate, prob, dh * act, side, gate * hidden, side], axis=1).astype(BF16)
            d_ref[e, h * HSLOTS:(h + 1) * HSLOTS, :] = d
            spread = dot(ones(slots == info[:, e:e + 1]), d[:, :PAIR])
            out_ref[:, e * PAIR:(e + 1) * PAIR] = spread.astype(BF16)
            mine = info == (first + e).astype(F32)
            mine = mine & (wide >= IDS_AT) & (wide < IDS_AT + TOP)
            tail = jnp.where(mine, spread[:, FSH:FSH + 1], tail)
        if h == 0:
            tail_ref[...] = tail
    tail = jnp.concatenate([tail, none], axis=1)
    copies[6].wait()
    for g in range(NG):
        give_ref[:, g] = dx_of(far_ref[...], wx_ref[g], tail).astype(BF16)


def input_kernel(*refs):
    dx_ref, spread_ref, tail_ref, wx_ref, got_ref, sems = refs[4:]
    for copy in fetch(refs[:4], (spread_ref, tail_ref, wx_ref, got_ref), sems):
        copy.wait()
    none = jnp.zeros((HALF, WIDE - LANES), F32)
    tail = jnp.concatenate([tail_ref[...], none], axis=1)
    for g in range(NG):
        dx = dx_of(spread_ref[...], wx_ref[g], tail) + got_ref[:, g].astype(F32)
        dx_ref[:, g] = dx.astype(BF16)


def weight_kernel(xs_ref, ds_ref, d_ref, out_ref):
    for e in range(NE):
        for g in range(NG):
            both = dot_dims(xs_ref[g, e], d_ref[e, :, :PAIR], 0, 0)
            down = dot_dims(ds_ref[g, e], d_ref[e, :, PAIR:], 0, 0)
            for i, (grad, base) in enumerate(((both, 0), (both, LANES), (down, 0))):
                pieces = [grad[s * STEP:s * STEP + Q, base:base + FSH] for s in range(4)]
                out_ref[g, e, i] = jnp.concatenate(pieces, axis=1).astype(BF16)


def finish_kernel(dx_any, got_any, in_ref, probs_ref, dx_ref, got_ref, sems):
    for copy in fetch((dx_any, got_any), (dx_ref, got_ref), sems):
        copy.wait()
    total = dx_ref[...] + got_ref[...].astype(F32)
    row, column = iota((WIDE, DSH), 0), iota((WIDE, DSH), 1)
    order = ones(feature_of(row) == column)
    in_ref[...] = dot(total.astype(BF16), order).astype(BF16)
    probs_ref[...] = total[:, :LANES].T[IDS_AT:IDS_AT + TOP, :]


def call(kernel, outs, args, scratch=(), scalar=False, by_hand=False, grant=VMEM):
    vmem = pl.BlockSpec(memory_space=pltpu.VMEM)
    specs = [pl.BlockSpec(memory_space=pl.ANY) if by_hand else vmem] * len(args)
    if scalar:
        specs[0] = pl.BlockSpec(memory_space=pltpu.SMEM)
    scratch_shapes = [pltpu.VMEM(shape, dtype) for shape, dtype in scratch]
    if by_hand:
        fetched = args[1:] if scalar else args
        scratch_shapes += [pltpu.VMEM(v.shape, v.dtype) for v in fetched]
        scratch_shapes.append(pltpu.SemaphoreType.DMA((len(fetched),)))
    return pl.pallas_call(
        kernel,
        out_shape=[jax.ShapeDtypeStruct(shape, dtype) for shape, dtype in outs],
        in_specs=specs,
        out_specs=[vmem] * len(outs),
        scratch_shapes=scratch_shapes,
        compiler_params=pltpu.CompilerParams(vmem_limit_bytes=grant),
    )(*args)


def exchange(value, axis):
    return lax.all_to_all(value, axis, split_axis=0, concat_axis=0, tiled=True)


def swap(value, axis):
    return lax.ppermute(value, axis, [(0, 1), (1, 0)])


def flip(value, axis, bit):
    return lax.ppermute(value, axis, [(i, i ^ bit) for i in range(lax.axis_size(axis))])


def local(stash, scale_exp, grad_out, route_ids, route_probs, w_gate, w_up, w_down):
    group = lax.axis_index(GROUP).astype(jnp.int32)
    zq = lax.axis_index("zq").astype(jnp.int32)
    me = jnp.stack([group] + [zq ^ s for s in range(4)])
    small = [v.T for v in (scale_exp, route_ids, route_probs)]
    (xin,) = call(prepare_kernel, [((SHARD, COLS), BF16)], (stash, small[0], grad_out, small[1], small[2]),
                  grant=MOST)
    with jax.named_scope("gather_tokens"):
        xin = jnp.concatenate([xin, swap(xin, "zh")])
        x0 = exchange(jnp.tile(xin, (NX * NG, 1)), ("x",) + GROUP).reshape(NX, NG, 2 * SHARD, COLS)
        x1 = swap(x0, "core")
    with jax.named_scope("move_weights"):
        tiles = [w.reshape(EXPERTS, 1, Q, 4 * FSH) for w in (w_gate, w_up, w_down)]
        weights, x0 = lax.optimization_barrier((jnp.concatenate(tiles, axis=1), x0))
        weights = exchange(weights, GROUP).reshape(NG, NE * 3 * Q, 4 * FSH)
    rows = ((NG, NE, SLOTS, WIDE), BF16)
    xs, ds, gate, slot = call(
        select_kernel,
        [rows, rows, ((NE, SLOTS, LANES), F32), ((TOKENS, LANES), F32)],
        (me, x0, x1),
        [((2, HALF, HALF), BF16)],
        True)
    part = ((PART, PACK), BF16)
    keep, give1, give2, give3, wx = call(
        forward_kernel,
        [((PART, PACK), F32), part, part, part, ((NG, WIDE, NE * PAIR), BF16)],
        (me, weights, xs, ds),
        [((NG, WIDE, NE * LANES), BF16), ((HSLOTS, PACK), F32)],
        True, True)
    with jax.named_scope("sum_pre"):
        got = [flip(give, "zq", 1 + i) for i, give in enumerate((give1, give2, give3))]
        pre = (keep + sum(v.astype(F32) for v in got)).astype(BF16)
    with jax.named_scope("spread_pre"):
        pre = [pre] + [flip(pre, "zq", s) for s in range(1, 4)]
    dx_shape = (NX, NG, SHARD, COLS)
    d, spread, tail, give = call(
        middle_kernel,
        [((NE, SLOTS, 3 * LANES), BF16), ((HALF, NE * PAIR), BF16), ((HALF, LANES), F32), (dx_shape, BF16)],
        (me, *pre, gate, slot, wx),
        [((HSLOTS, PACK), F32), ((HALF, NE * PAIR), BF16)],
        True, True)
    with jax.named_scope("sum_dx"):
        (dx,) = call(input_kernel, [(dx_shape, BF16)], (spread, tail, wx, swap(give, "core")), by_hand=True)
        dx, d = lax.optimization_barrier((dx, d))
        dx = exchange(dx.reshape(NX * NG, SHARD, COLS), ("x",) + GROUP)
        dx = jnp.sum(dx.astype(F32), axis=0)
        keep, give = dx[:, :WIDE], dx[:, WIDE:].astype(BF16)
    (grads,) = call(weight_kernel, [((NG, NE, 3, Q, 4 * FSH), BF16)], (xs, ds, d))
    give, grads = lax.optimization_barrier((give, grads))
    got = swap(give, "zh")
    with jax.named_scope("return_grads"):
        grads = exchange(grads.reshape(EXPERTS, 3, Q, 4 * FSH), GROUP)
        grads = [grads[:, i].reshape(w_gate.shape) for i in range(3)]
    keep, *grads = lax.optimization_barrier((keep, *grads))
    grad_in, grad_probs = call(finish_kernel, [((SHARD, DSH), BF16), ((TOP, SHARD), F32)], (keep, got), by_hand=True)
    return (grad_in, grad_probs.T, *grads)


def solution(mesh):
    fine = Mesh(mesh.devices.reshape(4, 2, 2, 4, 2, 4), DP + EX)
    weight = P(None, DP + EX)
    in_specs = (P(DP, EX), P(DP, EX), P(DP, EX), P(DP, None), P(DP, None), weight, weight, weight)
    out_specs = (P(DP, EX), P(DP, None), weight, weight, weight)
    return jax.shard_map(local, mesh=fine, in_specs=in_specs, out_specs=out_specs, check_vma=False)
```

```python
import jax
import jax.numpy as jnp
from jax import lax
from jax.experimental import pallas as pl
from jax.experimental.pallas import tpu as pltpu
from jax.sharding import Mesh, PartitionSpec as P

DP = ("x", "zh", "core")
EX = ("zq", "zp", "y")
GROUP = ("zp", "y")
BLK = 16
TOP = 6
CAP = 8
EXPERTS = 16
DSH = 160
FSH = 96
SHARD = 32
TOKENS = 512
BLOCKS = TOKENS // BLK
LANES = 128
NG = 8
NE = EXPERTS // NG
NX = 4
SLOTS = BLOCKS * CAP
HALF = TOKENS // 2
HSLOTS = SLOTS // 2
PART = HSLOTS // 4
Q = DSH // 4
STEP = Q + 8
WIDE = 4 * STEP
COLS = 2 * WIDE
IDS_AT = Q
PROBS_AT = STEP + Q
TRIO = 3 * FSH
PACK = 2 * NE * TRIO
PAIR = 2 * LANES
VMEM = 24 * 1024 * 1024
MOST = 56 * 1024 * 1024
BF16 = jnp.bfloat16
F32 = jnp.float32


def iota(shape, dim):
    return lax.broadcasted_iota(jnp.int32, shape, dim)


def dot(a, b):
    return jnp.dot(a, b, preferred_element_type=F32)


def dot_dims(a, b, left, right):
    return lax.dot_general(a, b, (((left,), (right,)), ((), ())), preferred_element_type=F32)


def fetch(sources, targets, sems):
    copies = [pltpu.make_async_copy(a, b, sems.at[i]) for i, (a, b) in enumerate(zip(sources, targets))]
    for copy in copies:
        copy.start()
    return copies


def feature_of(column):
    s = sum(jnp.where(column >= i * STEP, 1, 0) for i in range(1, 4))
    q = column - s * STEP
    return jnp.where((q < Q) & (column >= 0) & (column < WIDE), 4 * q + s, -1)


def ones(mask):
    return jnp.where(mask, 1.0, 0.0).astype(BF16)


def prepare_kernel(stash_ref, scale_ref, dy_ref, ids_ref, probs_ref, out_ref):
    scale = scale_ref[...]
    factor = jnp.where(scale == -2, 0.25, jnp.where(scale == -1, 0.5, jnp.where(scale == 0, 1.0, 2.0)))
    per = DSH // scale.shape[0]
    shape = (scale.shape[0], DSH)
    first = iota(shape, 0) * per
    expand = ones((iota(shape, 1) >= first) & (iota(shape, 1) < first + per))
    x = (stash_ref[...].astype(F32) * dot_dims(factor.astype(BF16), expand, 0, 0)).astype(BF16)
    row, column = iota((DSH, COLS), 0), iota((DSH, COLS), 1)
    out = dot(x, ones(row == feature_of(column)))
    out = out + dot(dy_ref[...], ones(row == feature_of(column - WIDE)))
    row, column = iota((TOP, COLS), 0), iota((TOP, COLS), 1)
    out = out + dot_dims(ids_ref[...].astype(F32).astype(BF16), ones(row == column - IDS_AT), 0, 0)
    out = out + dot_dims(probs_ref[...], ones(row == column - PROBS_AT), 0, 0)
    out_ref[...] = out.astype(BF16)


def repeat_kernel(own_ref, other_ref, out_ref):
    for i in range(NX * NG):
        out_ref[i, :SHARD] = own_ref[...]
        out_ref[i, SHARD:] = other_ref[...]


def select_kernel(me_ref, x0_ref, x1_ref, xs_ref, ds_ref, gate_ref, slot_ref, pick_ref):
    first = me_ref[0] * NE
    lane = iota((HALF, LANES), 1)
    row, column = iota((HALF, HALF), 0), iota((HALF, HALF), 1)
    before = ones((column < row) & (column >= row - row % BLK))
    block = (iota((HALF, LANES), 0) // BLK).astype(F32)
    row = iota((HSLOTS, HALF), 0).astype(F32)

    def tokens(x_ref, g, lanes):
        return x_ref[:, g, :, lanes].reshape(HALF, lanes.stop - lanes.start)

    for h, x_ref in enumerate((x0_ref, x1_ref)):
        at = slice(h * HALF, (h + 1) * HALF)
        head = tokens(x_ref, 0, slice(0, LANES)).astype(F32)
        hit = jnp.zeros((HALF, LANES), F32)
        prob = jnp.zeros((HALF, LANES), F32)
        for k in range(TOP):
            same = head[:, IDS_AT + k:IDS_AT + k + 1] == (lane + first).astype(F32)
            hit = jnp.where(same, 1.0, hit)
            prob = jnp.where(same, head[:, PROBS_AT + k:PROBS_AT + k + 1], prob)
        place = dot(before, hit.astype(BF16))
        slot = jnp.where(hit > 0.5, block * CAP + place, -1.0)
        slot_ref[at, :] = jnp.where(lane < NE, slot, head)
        slot_t = slot.T
        for e in range(NE):
            pick_ref[h, e * HSLOTS:(e + 1) * HSLOTS, :] = ones(row == slot_t[e:e + 1, :])
        gate = dot(pick_ref[h], prob.astype(BF16))
        for e in range(NE):
            gate_ref[e, h * HSLOTS:(h + 1) * HSLOTS, :] = gate[e * HSLOTS:(e + 1) * HSLOTS]
    for g in range(NG):
        for h, x_ref in enumerate((x0_ref, x1_ref)):
            x = dot(pick_ref[h], tokens(x_ref, g, slice(0, WIDE))).astype(BF16)
            dy = dot(pick_ref[h], tokens(x_ref, g, slice(WIDE, COLS))).astype(BF16)
            at = slice(h * HSLOTS, (h + 1) * HSLOTS)
            for e in range(NE):
                xs_ref[g, e, at, :] = x[e * HSLOTS:(e + 1) * HSLOTS]
                ds_ref[g, e, at, :] = dy[e * HSLOTS:(e + 1) * HSLOTS]


def forward_kernel(me_ref, *refs):
    (keep_ref, give1_ref, give2_ref, give3_ref, wx_ref, wd_ref, pre_ref, w_ref, xs_ref, ds_ref, sems) = refs[3:]
    copies = fetch(refs[:3], (w_ref, xs_ref, ds_ref), sems)
    copies[0].wait()
    low = jnp.zeros((STEP - Q, FSH), F32)
    side = jnp.zeros((STEP, LANES - FSH), F32)
    for g in range(NG):
        every = w_ref[g].astype(F32)
        for e in range(NE):
            for i in range(3):
                w = every[(3 * e + i) * Q:(3 * e + i + 1) * Q]
                for s in range(4):
                    piece = jnp.concatenate([w[:, s * FSH:(s + 1) * FSH], low], axis=0)
                    piece = jnp.concatenate([piece, side], axis=1).astype(BF16)
                    if i < 2:
                        wx_ref[g, s * STEP:(s + 1) * STEP, e * PAIR + i * LANES:e * PAIR + (i + 1) * LANES] = piece
                    else:
                        wd_ref[g, s * STEP:(s + 1) * STEP, e * LANES:(e + 1) * LANES] = piece
    copies[1].wait()
    copies[2].wait()
    for e in range(NE):
        ab = jnp.zeros((SLOTS, PAIR), F32)
        back = jnp.zeros((SLOTS, LANES), F32)
        for g in range(NG):
            ab = ab + dot(xs_ref[g, e], wx_ref[g, :, e * PAIR:(e + 1) * PAIR])
            back = back + dot(ds_ref[g, e], wd_ref[g, :, e * LANES:(e + 1) * LANES])
        trio = jnp.concatenate([ab[:, :FSH], ab[:, LANES:LANES + FSH], back[:, :FSH]], axis=1)
        for h in range(2):
            unit = 2 * e + h
            pre_ref[:, unit * TRIO:(unit + 1) * TRIO] = trio[h * HSLOTS:(h + 1) * HSLOTS]
    for s, out_ref in enumerate((keep_ref, give1_ref, give2_ref, give3_ref)):
        rows = pl.ds(pl.multiple_of(me_ref[1 + s] * PART, PART), PART)
        out_ref[...] = pre_ref[rows, :].astype(out_ref.dtype)


def dx_of(spread, wx, tail):
    dx = dot_dims(spread, wx, 1, 1) + tail
    dx = dx.reshape(NX, 2, SHARD, WIDE)
    return jnp.concatenate([dx[:, 0], dx[:, 1]], axis=2)


def middle_kernel(me_ref, *refs):
    (d_ref, spread_ref, tail_ref, give_ref, pre_ref, far_ref, *local_refs, sems) = refs[7:]
    (gate_ref, slot_ref, wx_ref), parts = local_refs[4:], local_refs[:4]
    copies = fetch(refs[:7], local_refs, sems)
    first = me_ref[0] * NE
    for s, part_ref in enumerate(parts):
        rows = pl.ds(pl.multiple_of(me_ref[1 + s] * PART, PART), PART)
        copies[s].wait()
        pre_ref[rows, :] = part_ref[...].astype(F32)
    copies[4].wait()
    copies[5].wait()
    side = jnp.zeros((HSLOTS, LANES - FSH), F32)
    lane = iota((HSLOTS, LANES - FSH), 1)
    slots = iota((HALF, HSLOTS), 1).astype(F32)
    wide = iota((HALF, LANES), 1)
    none = jnp.zeros((HALF, WIDE - LANES), F32)
    for h, out_ref in enumerate((spread_ref, far_ref)):
        info = slot_ref[h * HALF:(h + 1) * HALF, :]
        tail = jnp.zeros((HALF, LANES), F32)
        for e in range(NE):
            base = (2 * e + h) * TRIO
            pre = pre_ref[:, base:base + TRIO]
            a, b, back = (pre[:, i * FSH:(i + 1) * FSH] for i in range(3))
            gate = gate_ref[e, h * HSLOTS:(h + 1) * HSLOTS, e:e + 1]
            sig = jax.nn.sigmoid(a)
            act = a * sig
            hidden = act * b
            dh = gate * back
            d_gate = dh * b * sig * (1.0 + a * (1.0 - sig))
            prob = jnp.sum(hidden * back, axis=1, keepdims=True)
            prob = jnp.where(lane == 0, prob, 0.0)
            d = jnp.concatenate([d_gate, prob, dh * act, side, gate * hidden, side], axis=1).astype(BF16)
            d_ref[e, h * HSLOTS:(h + 1) * HSLOTS, :] = d
            spread = dot(ones(slots == info[:, e:e + 1]), d[:, :PAIR])
            out_ref[:, e * PAIR:(e + 1) * PAIR] = spread.astype(BF16)
            mine = info == (first + e).astype(F32)
            mine = mine & (wide >= IDS_AT) & (wide < IDS_AT + TOP)
            tail = jnp.where(mine, spread[:, FSH:FSH + 1], tail)
        if h == 0:
            tail_ref[...] = tail
    tail = jnp.concatenate([tail, none], axis=1)
    copies[6].wait()
    for g in range(NG):
        give_ref[:, g] = dx_of(far_ref[...], wx_ref[g], tail).astype(BF16)


def input_kernel(*refs):
    dx_ref, spread_ref, tail_ref, wx_ref, got_ref, sems = refs[4:]
    for copy in fetch(refs[:4], (spread_ref, tail_ref, wx_ref, got_ref), sems):
        copy.wait()
    none = jnp.zeros((HALF, WIDE - LANES), F32)
    tail = jnp.concatenate([tail_ref[...], none], axis=1)
    for g in range(NG):
        dx = dx_of(spread_ref[...], wx_ref[g], tail) + got_ref[:, g].astype(F32)
        dx_ref[:, g] = dx.astype(BF16)


def weight_kernel(xs_ref, ds_ref, d_ref, out_ref):
    for e in range(NE):
        for g in range(NG):
            both = dot_dims(xs_ref[g, e], d_ref[e, :, :PAIR], 0, 0)
            down = dot_dims(ds_ref[g, e], d_ref[e, :, PAIR:], 0, 0)
            for i, (grad, base) in enumerate(((both, 0), (both, LANES), (down, 0))):
                pieces = [grad[s * STEP:s * STEP + Q, base:base + FSH] for s in range(4)]
                out_ref[g, e, i] = jnp.concatenate(pieces, axis=1).astype(BF16)


def finish_kernel(dx_any, got_any, in_ref, probs_ref, dx_ref, got_ref, sems):
    for copy in fetch((dx_any, got_any), (dx_ref, got_ref), sems):
        copy.wait()
    total = dx_ref[...] + got_ref[...].astype(F32)
    row, column = iota((WIDE, DSH), 0), iota((WIDE, DSH), 1)
    order = ones(feature_of(row) == column)
    in_ref[...] = dot(total.astype(BF16), order).astype(BF16)
    probs_ref[...] = total[:, :LANES].T[IDS_AT:IDS_AT + TOP, :]


def call(kernel, outs, args, scratch=(), scalar=False, by_hand=False, grant=VMEM):
    vmem = pl.BlockSpec(memory_space=pltpu.VMEM)
    specs = [pl.BlockSpec(memory_space=pl.ANY) if by_hand else vmem] * len(args)
    if scalar:
        specs[0] = pl.BlockSpec(memory_space=pltpu.SMEM)
    scratch_shapes = [pltpu.VMEM(shape, dtype) for shape, dtype in scratch]
    if by_hand:
        fetched = args[1:] if scalar else args
        scratch_shapes += [pltpu.VMEM(v.shape, v.dtype) for v in fetched]
        scratch_shapes.append(pltpu.SemaphoreType.DMA((len(fetched),)))
    return pl.pallas_call(
        kernel,
        out_shape=[jax.ShapeDtypeStruct(shape, dtype) for shape, dtype in outs],
        in_specs=specs,
        out_specs=[vmem] * len(outs),
        scratch_shapes=scratch_shapes,
        compiler_params=pltpu.CompilerParams(vmem_limit_bytes=grant),
    )(*args)


def exchange(value, axis):
    return lax.all_to_all(value, axis, split_axis=0, concat_axis=0, tiled=True)


def swap(value, axis):
    return lax.ppermute(value, axis, [(0, 1), (1, 0)])


def flip(value, axis, bit):
    return lax.ppermute(value, axis, [(i, i ^ bit) for i in range(lax.axis_size(axis))])


def local(stash, scale_exp, grad_out, route_ids, route_probs, w_gate, w_up, w_down):
    group = lax.axis_index(GROUP).astype(jnp.int32)
    zq = lax.axis_index("zq").astype(jnp.int32)
    me = jnp.stack([group] + [zq ^ s for s in range(4)])
    small = [v.T for v in (scale_exp, route_ids, route_probs)]
    (xin,) = call(prepare_kernel, [((SHARD, COLS), BF16)], (stash, small[0], grad_out, small[1], small[2]),
                  grant=MOST)
    with jax.named_scope("gather_tokens"):
        (xin,) = call(repeat_kernel, [((NX * NG, 2 * SHARD, COLS), BF16)], (xin, swap(xin, "zh")), grant=MOST)
        x0 = exchange(xin, ("x",) + GROUP).reshape(NX, NG, 2 * SHARD, COLS)
        x1 = swap(x0, "core")
    with jax.named_scope("move_weights"):
        tiles = [w.reshape(EXPERTS, 1, Q, 4 * FSH) for w in (w_gate, w_up, w_down)]
        weights, x0 = lax.optimization_barrier((jnp.concatenate(tiles, axis=1), x0))
        weights = exchange(weights, GROUP).reshape(NG, NE * 3 * Q, 4 * FSH)
    rows = ((NG, NE, SLOTS, WIDE), BF16)
    xs, ds, gate, slot = call(
        select_kernel,
        [rows, rows, ((NE, SLOTS, LANES), F32), ((TOKENS, LANES), F32)],
        (me, x0, x1),
        [((2, HALF, HALF), BF16)],
        True)
    part = ((PART, PACK), BF16)
    keep, give1, give2, give3, wx = call(
        forward_kernel,
        [((PART, PACK), F32), part, part, part, ((NG, WIDE, NE * PAIR), BF16)],
        (me, weights, xs, ds),
        [((NG, WIDE, NE * LANES), BF16), ((HSLOTS, PACK), F32)],
        True, True)
    with jax.named_scope("sum_pre"):
        got = [flip(give, "zq", 1 + i) for i, give in enumerate((give1, give2, give3))]
        pre = (keep + sum(v.astype(F32) for v in got)).astype(BF16)
    with jax.named_scope("spread_pre"):
        pre = [pre] + [flip(pre, "zq", s) for s in range(1, 4)]
    dx_shape = (NX, NG, SHARD, COLS)
    d, spread, tail, give = call(
        middle_kernel,
        [((NE, SLOTS, 3 * LANES), BF16), ((HALF, NE * PAIR), BF16), ((HALF, LANES), F32), (dx_shape, BF16)],
        (me, *pre, gate, slot, wx),
        [((HSLOTS, PACK), F32), ((HALF, NE * PAIR), BF16)],
        True, True)
    with jax.named_scope("sum_dx"):
        (dx,) = call(input_kernel, [(dx_shape, BF16)], (spread, tail, wx, swap(give, "core")), by_hand=True)
        dx, d = lax.optimization_barrier((dx, d))
        dx = exchange(dx.reshape(NX * NG, SHARD, COLS), ("x",) + GROUP)
        dx = jnp.sum(dx.astype(F32), axis=0)
        keep, give = dx[:, :WIDE], dx[:, WIDE:].astype(BF16)
    (grads,) = call(weight_kernel, [((NG, NE, 3, Q, 4 * FSH), BF16)], (xs, ds, d))
    give, grads = lax.optimization_barrier((give, grads))
    got = swap(give, "zh")
    with jax.named_scope("return_grads"):
        grads = exchange(grads.reshape(EXPERTS, 3, Q, 4 * FSH), GROUP)
        grads = [grads[:, i].reshape(w_gate.shape) for i in range(3)]
    keep, *grads = lax.optimization_barrier((keep, *grads))
    grad_in, grad_probs = call(finish_kernel, [((SHARD, DSH), BF16), ((TOP, SHARD), F32)], (keep, got), by_hand=True)
    return (grad_in, grad_probs.T, *grads)


def solution(mesh):
    fine = Mesh(mesh.devices.reshape(4, 2, 2, 4, 2, 4), DP + EX)
    weight = P(None, DP + EX)
    in_specs = (P(DP, EX), P(DP, EX), P(DP, EX), P(DP, None), P(DP, None), weight, weight, weight)
    out_specs = (P(DP, EX), P(DP, None), weight, weight, weight)
    return jax.shard_map(local, mesh=fine, in_specs=in_specs, out_specs=out_specs, check_vma=False)
```
